32 devices in a mesh: farm: 2 (over x), blk: 16 (over z, y, core).
Axes of the slice: x: 2, y: 2, z: 4, core: 2. Of those that a mesh axis runs over, the one named last changes fastest.
Arguments:
- particle_pos: float32 [3, 65536], P(None, ('farm', 'blk')), parts along dimension 1, may hold values from -2 to 2
- vorticity: float32 [3, 65536], P(None, ('farm', 'blk')), parts along dimension 1, may hold values from -6 to 6
- particle_owner: int32 [65536], P(('farm', 'blk')), parts along dimension 0, may hold values from 0 to 15, as said below
- thrust_coef: float32 [32], P('farm'), parts along dimension 0, may hold values from 0.3 to 1
- node_pos: float32 [3, 4096], P(None, ('farm', 'blk')), parts along dimension 1, may hold values from -2 to 2
- lever_arm: float32 [3, 4096], P(None, ('farm', 'blk')), parts along dimension 1, may hold values from -1 to 1
- chord_coef: float32 [4096], P(('farm', 'blk')), parts along dimension 0, may hold values from 0.005 to 0.02
- node_platform: int32 [4096], P(('farm', 'blk')), parts along dimension 0, may hold values from 0 to 15, as said below
- platform_pos: float32 [6, 32], P(None, ('farm', 'blk')), parts along dimension 1, may hold values from -0.3 to 0.3
- platform_vel: float32 [6, 32], P(None, ('farm', 'blk')), parts along dimension 1, may hold values from -1.5 to 1.5
- velocity_history: float32 [32, 6, 1024], P(('farm', 'blk')), parts along dimension 0, may hold values from -6 to 6
- memory_kernel: float32 [6, 6, 1024], replicated, may hold values from -0.078125 to 0.078125
- restoring: float32 [6], replicated, may hold values from 1 to 4
- inverse_mass: float32 [6, 6], replicated, may hold values from -0.15 to 1, as said below
- line_offset: float32 [3, 96, 128], P(None, ('farm', 'blk')), parts along dimension 1, may hold values from -0.3125 to 0.3125
- line_velocity: float32 [3, 96, 128], P(None, ('farm', 'blk')), parts along dimension 1, may hold values from -6 to 6
- line_platform: int32 [96], P(('farm', 'blk')), parts along dimension 0, may hold values from 0 to 15, as said below
Outputs:
- induced_velocity: float32 [3, 65536], P(None, ('farm', 'blk')), parts along dimension 1
- platform_accel: float32 [6, 32], P(None, ('farm', 'blk')), parts along dimension 1
- line_accel: float32 [3, 96, 128], P(None, ('farm', 'blk')), parts along dimension 1
The draws below stay inside these ranges and needn't reach their ends.
There are 2 independent parts, one for each index of `farm`. The reference program is written for one: setup_inputs(seed, part) draws one part's arguments, and reference() takes and returns one part's arrays. A program takes and returns all parts, laid end to end along the dimension named above; an argument that names none is the same for every part. Nothing has to cross between parts.
Inputs may be any that keep to these rules, and one draw needn't show every extreme that they name: `particle_owner`: each turbine shed exactly 2048 particles. `node_platform`: each platform carries exactly 128 nodes. `line_platform`: each platform holds exactly 3 lines. `inverse_mass`: diagonal between 0.5 and 1, other entries between -0.15 and 0.15.
All inputs are finite; a program needn't handle non-finite values.
Results may differ from the reference program's by a relative error of at most 0.0003.
Values sent between devices are 32-bit elements; how exact they have to be, the bound alone decides.
No kernel may reach another device: no remote copies, remote signals or barrier semaphores. Data moves between devices by JAX's collectives and lax.ppermute only.
A program may use at most 64 MiB of HBM per device.

```python
import math
import jax
import jax.numpy as jnp
from jax import lax

PART_DEV = 2048
NODE_DEV = 128
LAGS = 1024
SEGS = 128
PARTICLES = 32768
NODES = 2048
PLATFORMS = 16
LINES = 48
N_BLK = 16


def draw_particle_owner(key, part):
    key = jax.random.fold_in(key, 11)
    base = jnp.arange(PARTICLES, dtype=jnp.int32) % PLATFORMS
    return jax.random.permutation(key, base).astype(jnp.int32)


def draw_node_platform(key, part):
    key = jax.random.fold_in(key, 13)
    base = jnp.arange(NODES, dtype=jnp.int32) % PLATFORMS
    return jax.random.permutation(key, base).astype(jnp.int32)


def draw_line_platform(key, part):
    key = jax.random.fold_in(key, 17)
    base = jnp.arange(LINES, dtype=jnp.int32) // 3
    return jax.random.permutation(key, base).astype(jnp.int32)


def draw_inverse_mass(key, part):
    key = jax.random.fold_in(key, 19)
    first_key, second_key = jax.random.split(key)
    outside = jax.random.uniform(first_key, (6, 6), jnp.float32, -0.15, 0.15)
    diagonal = jax.random.uniform(second_key, (6,), jnp.float32, 0.5, 1.0)
    identity = jnp.eye(6, dtype=jnp.float32)
    return outside * (1.0 - identity) + identity * diagonal[None, :]


def draw_platform_pos(key, part):
    key = jax.random.fold_in(key, 23)
    values = jnp.clip(0.1 * jax.random.normal(key, (6, PLATFORMS), jnp.float32), -0.3, 0.3)
    return values.astype(jnp.float32)


def steps_of(stream_key, shape, cuts, low, largest):
    def one(position, shards_of):
        heights = jax.random.uniform(jax.random.fold_in(jax.random.fold_in(stream_key, 6), position), (shards_of,), jnp.float32, low / len(cuts), largest / len(cuts))
        return jnp.repeat(jnp.exp(heights), shape[position] // shards_of).reshape((-1,) + (1,) * (len(shape) - position - 1))

    level = one(*cuts[0])
    for cut in cuts[1:]:
        level = level * one(*cut)
    return level


def normal_values(stream_key, extent, deviation, bound, pieces=(), kind=jnp.bfloat16):
    gain = steps_of(stream_key, extent, pieces, -0.22, 0.18) if pieces else 1.0
    result = jax.random.normal(stream_key, extent, jnp.float32) * deviation * gain
    return jnp.minimum(jnp.maximum(result, -bound), bound).astype(kind)


def setup_inputs(seed: int = 0, part: int = 0) -> dict:
    keys = jax.random.split(jax.random.key(seed), 18)
    own_keys = jax.random.split(jax.random.fold_in(keys[17], part), 18)
    particle_pos = jnp.clip(jax.random.uniform(own_keys[0], (3, PARTICLES), jnp.float32, -2.0, 2.0) * steps_of(own_keys[0], (3, PARTICLES), ((1, 16),), -0.4, 0.0), -2.0, 2.0)
    vorticity = normal_values(own_keys[1], (3, PARTICLES), 1.0, 6.0, ((1, 16),), jnp.float32)
    particle_owner = draw_particle_owner(jax.random.fold_in(jax.random.fold_in(keys[17], part), 71), part)
    thrust_coef = jnp.clip(jnp.exp(jax.random.uniform(own_keys[3], (PLATFORMS,), jnp.float32, math.log(0.3), math.log(1.0))), 0.3, 1.0)
    node_pos = jnp.clip(jax.random.uniform(own_keys[4], (3, NODES), jnp.float32, -2.0, 2.0) * steps_of(own_keys[4], (3, NODES), ((1, 16),), -0.4, 0.0), -2.0, 2.0)
    lever_arm = jnp.clip(jax.random.uniform(own_keys[5], (3, NODES), jnp.float32, -1.0, 1.0) * steps_of(own_keys[5], (3, NODES), ((1, 16),), -0.4, 0.0), -1.0, 1.0)
    chord_coef = jnp.clip(jnp.exp(math.log(0.02) - 1.3862944 * jax.random.uniform(own_keys[6], (NODES,), jnp.float32) ** steps_of(own_keys[6], (NODES,), ((0, 16),), -0.2, 0.2)), 0.005, 0.02)
    node_platform = draw_node_platform(jax.random.fold_in(jax.random.fold_in(keys[17], part), 71), part)
    platform_pos = draw_platform_pos(jax.random.fold_in(jax.random.fold_in(keys[17], part), 71), part)
    platform_vel = normal_values(own_keys[9], (6, PLATFORMS), 0.1, 1.5, ((1, 16),), jnp.float32)
    velocity_history = normal_values(own_keys[10], (PLATFORMS, 6, LAGS), 1.0, 6.0, ((0, 16),), jnp.float32)
    memory_kernel = normal_values(keys[11], (6, 6, LAGS), (6 * LAGS) ** -0.5, 0.078125, (), jnp.float32)
    restoring = jnp.clip(jnp.exp(jax.random.uniform(keys[12], (6,), jnp.float32, math.log(1.0), math.log(4.0))), 1.0, 4.0)
    inverse_mass = draw_inverse_mass(jax.random.fold_in(keys[17], 71), part)
    line_offset = normal_values(own_keys[14], (3, LINES, SEGS), 0.02, 0.3125, ((1, 16),), jnp.float32)
    line_velocity = normal_values(own_keys[15], (3, LINES, SEGS), 1.0, 6.0, ((1, 16),), jnp.float32)
    line_platform = draw_line_platform(jax.random.fold_in(jax.random.fold_in(keys[17], part), 71), part)
    return {"particle_pos": particle_pos, "vorticity": vorticity, "particle_owner": particle_owner, "thrust_coef": thrust_coef, "node_pos": node_pos, "lever_arm": lever_arm, "chord_coef": chord_coef, "node_platform": node_platform, "platform_pos": platform_pos, "platform_vel": platform_vel, "velocity_history": velocity_history, "memory_kernel": memory_kernel, "restoring": restoring, "inverse_mass": inverse_mass, "line_offset": line_offset, "line_velocity": line_velocity, "line_platform": line_platform}


core_square = 0.01
inverse_four_pi = 0.25 / math.pi
line_spacing = 1.0
rest_length = 0.95 * math.sqrt(1.36)
line_stiffness = 20.0
node_weight = 0.5
line_damping = 0.5
high_precision = lax.Precision.HIGHEST

def cross_product(first, second):
    return jnp.stack([first[1] * second[2] - first[2] * second[1], first[2] * second[0] - first[0] * second[2], first[0] * second[1] - first[1] * second[0]])

def induced(targets, sources, strengths, block_len):
    blocks_in = sources.shape[1] // block_len
    source_blocks = sources.reshape(3, blocks_in, block_len).transpose(1, 0, 2)
    strength_blocks = strengths.reshape(3, blocks_in, block_len).transpose(1, 0, 2)

    def advance(running, block_pair):
        where_from, circulation = block_pair
        sep_x = targets[0][:, None] - where_from[0][None, :]
        sep_y = targets[1][:, None] - where_from[1][None, :]
        sep_z = targets[2][:, None] - where_from[2][None, :]
        dist_sq = sep_x * sep_x + sep_y * sep_y + sep_z * sep_z + core_square
        kernel_value = lax.rsqrt(dist_sq) / dist_sq * inverse_four_pi
        vel_x = lax.optimization_barrier(jnp.sum(kernel_value * (circulation[1][None, :] * sep_z - circulation[2][None, :] * sep_y), axis=1))
        vel_y = lax.optimization_barrier(jnp.sum(kernel_value * (circulation[2][None, :] * sep_x - circulation[0][None, :] * sep_z), axis=1))
        vel_z = lax.optimization_barrier(jnp.sum(kernel_value * (circulation[0][None, :] * sep_y - circulation[1][None, :] * sep_x), axis=1))
        return (running + jnp.stack([vel_x, vel_y, vel_z]), None)
    running, unused = lax.scan(advance, jnp.zeros(targets.shape, jnp.float32), (source_blocks, strength_blocks))
    return running

def blade_terms(node_induced, node_motion, lever_arm, chord_coef):
    rigid = node_motion[:3] + cross_product(node_motion[3:], lever_arm)
    stream = jnp.array([1.0, 0.0, 0.0], jnp.float32)[:, None]
    relative = stream + node_induced - rigid
    magnitude = jnp.sqrt(lax.optimization_barrier(jnp.sum(relative * relative, axis=0)))
    node_force = (chord_coef * magnitude)[None, :] * relative
    return jnp.concatenate([node_force, cross_product(lever_arm, node_force)], axis=0)

def mooring(line_offset, line_velocity, line_index, fairlead):
    bearing = 2.0 * math.pi / 3.0 * (line_index % 3).astype(jnp.float32)
    heading = jnp.stack([jnp.cos(bearing), jnp.sin(bearing), jnp.full(bearing.shape, 0.6, jnp.float32)])
    segments_total = line_offset.shape[2]
    depth_steps = (segments_total - jnp.arange(segments_total)).astype(jnp.float32)
    positions = -line_spacing * heading[:, :, None] * depth_steps[None, None, :] + line_offset
    following = jnp.concatenate([positions[:, :, 1:], fairlead[:, :, None]], axis=2)
    segment = following - positions
    lengths = jnp.sqrt(lax.optimization_barrier(jnp.sum(segment * segment, axis=0)))
    tension = line_stiffness * (lengths - rest_length) / rest_length
    pull = (tension / lengths)[None] * segment
    previous = jnp.concatenate([jnp.zeros_like(pull[:, :, :1]), pull[:, :, :-1]], axis=2)
    gravity = jnp.array([0.0, 0.0, -node_weight], jnp.float32)[:, None, None]
    node_force = pull - previous + gravity - line_damping * line_velocity
    movable = (jnp.arange(segments_total) > 0).astype(jnp.float32)
    return (node_force * movable[None, None, :], -pull[:, :, -1])

def reference(particle_pos, vorticity, particle_owner, thrust_coef, node_pos, lever_arm, chord_coef, node_platform, platform_pos, platform_vel, velocity_history, memory_kernel, restoring, inverse_mass, line_offset, line_velocity, line_platform):
    strength_scale = thrust_coef[particle_owner] * (1.0 - platform_vel[0][particle_owner])
    strengths = vorticity * strength_scale[None, :]
    node_shift = platform_pos[:, node_platform]
    node_motion = platform_vel[:, node_platform]
    current = node_pos + node_shift[:3]
    grouped = jnp.concatenate([particle_pos.reshape(3, N_BLK, PART_DEV), current.reshape(3, N_BLK, NODE_DEV)], axis=2).transpose(1, 0, 2)
    velocity = lax.map(lambda group_targets: induced(group_targets, particle_pos, strengths, PART_DEV), grouped)
    induced_velocity = velocity[:, :, :PART_DEV].transpose(1, 0, 2).reshape(3, PARTICLES)
    node_induced = velocity[:, :, PART_DEV:].transpose(1, 0, 2).reshape(3, NODES)
    node_terms = blade_terms(node_induced, node_motion, lever_arm, chord_coef)
    line_index = jnp.arange(LINES, dtype=jnp.int32)
    fairlead = platform_pos[:3, line_platform]
    line_accel, fairlead_pull = mooring(line_offset, line_velocity, line_index, fairlead)
    line_terms = jnp.concatenate([fairlead_pull, jnp.zeros_like(fairlead_pull)], axis=0)
    loads = jax.ops.segment_sum(node_terms.T, node_platform, PLATFORMS).T
    loads = loads + jax.ops.segment_sum(line_terms.T, line_platform, PLATFORMS).T
    radiation = -jnp.einsum('ijk,pjk->ip', memory_kernel, velocity_history, precision=high_precision)
    total = loads + radiation - restoring[:, None] * platform_pos
    platform_accel = jnp.dot(inverse_mass, total, precision=high_precision)
    return (induced_velocity, platform_accel, line_accel)
```

```python
import functools
import math

import jax
import jax.numpy as jnp
import numpy as np
from jax import lax
from jax.experimental import pallas as pl
from jax.experimental.pallas import tpu as pltpu
from jax.sharding import PartitionSpec as P

core_square = 0.01
inverse_four_pi = 0.25 / math.pi
line_spacing = 1.0
rest_length = 0.95 * math.sqrt(1.36)
line_stiffness = 20.0
node_weight = 0.5
line_damping = 0.5
F32 = jnp.float32
BF16 = jnp.bfloat16
LANES = 128
TILE = 256
QUARTERS = 4
FEATURES = 32
third_turn = np.float32(2.0 * math.pi / 3.0)
cosines = [float(np.cos(third_turn * np.float32(k))) for k in range(3)]
sines = [float(np.sin(third_turn * np.float32(k))) for k in range(3)]


def piece(values):
    return values.astype(BF16).astype(F32)


def coordinate_pieces(pos, extra):
    first = jnp.round(pos * 64.0) * (1.0 / 64.0)
    rest = pos - first
    second = jnp.round(rest * 16384.0) * (1.0 / 16384.0)
    third = piece(rest - second)
    square = first * first
    norm = square[0:1] + square[1:2] + square[2:3]
    cross = rest * (pos + first)
    small = cross[0:1] + cross[1:2] + cross[2:3] + extra
    norm_a = piece(norm)
    norm_b = norm - norm_a
    small_a = piece(small)
    small_b = small - small_a
    return first, second, third, norm_a, norm_b, small_a, small_b


def source_rows(pos):
    first, second, third, norm_a, norm_b, small_a, small_b = coordinate_pieces(pos, 0.0)
    one = jnp.ones_like(norm_a)
    return jnp.concatenate(
        [first, norm_a, one, norm_b, one, small_a, one, first, second, small_b, one]
        + [second, first, third, second, third],
        axis=0,
    )


def target_rows(pos):
    first, second, third, norm_a, norm_b, small_a, small_b = coordinate_pieces(pos, core_square)
    one = jnp.ones_like(norm_a)
    first, second, third = -2.0 * first, -2.0 * second, -2.0 * third
    return jnp.concatenate(
        [first, one, norm_a, one, norm_b, one, small_a, second, first, one, small_b]
        + [second, third, first, third, second],
        axis=0,
    )


def strength_rows(block, scales):
    pos, vorticity, owner = block[0:3], block[3:6], block[6:7]
    scale = jnp.zeros_like(owner)
    for index, value in enumerate(scales):
        scale = jnp.where(owner == float(index), value, scale)
    strength = vorticity * scale
    s_hi = piece(strength)
    s_lo = piece(strength - s_hi)
    held = s_hi + s_lo
    moment = jnp.concatenate(
        [
            held[1:2] * pos[2:3] - held[2:3] * pos[1:2],
            held[2:3] * pos[0:1] - held[0:1] * pos[2:3],
            held[0:1] * pos[1:2] - held[1:2] * pos[0:1],
        ],
        axis=0,
    )
    m_hi = piece(moment)
    m_mid = piece(moment - m_hi)
    m_lo = moment - m_hi - m_mid
    return jnp.concatenate([s_hi, s_lo, m_hi, m_mid, m_lo, jnp.zeros_like(owner)], axis=0)


def step_kernel(
    chunk,
    me_ref,
    table_ref,
    thrust_ref,
    restoring_ref,
    mass_ref,
    line_platform_ref,
    misc_ref,
    pos_ref,
    blocks_ref,
    history_ref,
    memory_ref,
    offset_ref,
    line_velocity_ref,
    induced_ref,
    accel_ref,
    line_accel_ref,
    rows_ref,
    weights_ref,
    targets_ref,
    target_pos_ref,
    even_ref,
    odd_ref,
    sums_ref,
):
    devices = misc_ref.shape[0]
    platforms = thrust_ref.shape[0]
    blocks = blocks_ref.shape[0]
    own_count = pos_ref.shape[1]
    quarter = own_count // QUARTERS
    tiles = own_count // TILE + 1
    me = me_ref[0]

    on_platform = misc_ref[:, 7, :] == me.astype(F32)
    mark = on_platform.astype(F32)
    upper = lax.broadcasted_iota(jnp.int32, (LANES, LANES), 0) <= lax.broadcasted_iota(
        jnp.int32, (LANES, LANES), 1
    )
    counted = jnp.dot(mark.astype(BF16), upper.astype(F32).astype(BF16), preferred_element_type=F32)
    below = lax.broadcasted_iota(jnp.int32, (devices, devices), 0) > lax.broadcasted_iota(
        jnp.int32, (devices, devices), 1
    )
    totals = jnp.broadcast_to(counted[:, LANES - 1 :], counted.shape)
    before = jnp.dot(below.astype(F32).astype(BF16), totals.astype(BF16), preferred_element_type=F32)
    rank = jnp.where(on_platform, counted - 1.0 + before, -1.0)
    slots = lax.broadcasted_iota(jnp.int32, (LANES, LANES), 0).astype(F32)
    picked = jnp.zeros((24, LANES), F32)
    for device in range(devices):
        data = misc_ref[device, 0:8, :]
        hi = piece(data)
        mid = piece(data - hi)
        pieces = jnp.concatenate([hi, mid, data - hi - mid], axis=0).astype(BF16)
        pick = (slots == rank[device : device + 1]).astype(F32).astype(BF16)
        picked = picked + lax.dot_general(
            pieces, pick, (((1,), (1,)), ((), ())), preferred_element_type=F32
        )
    nodes = picked[0:8] + picked[8:16] + picked[16:24]
    current = jnp.concatenate([nodes[c : c + 1] + table_ref[0, c] for c in range(3)], axis=0)

    target_pos_ref[:, 0:own_count] = pos_ref[...]
    target_pos_ref[:, own_count : own_count + LANES] = current
    target_pos_ref[:, own_count + LANES :] = current
    for tile in range(tiles):
        features = target_rows(target_pos_ref[:, tile * TILE : (tile + 1) * TILE]).astype(BF16)
        for part in range(QUARTERS):
            slot = targets_ref.at[tile * QUARTERS + part]
            slot[...] = jnp.zeros((LANES, TILE), BF16)
            slot[part * FEATURES : (part + 1) * FEATURES, :] = features
        sums_ref[tile] = jnp.zeros((16, TILE), F32)

    scales = [
        thrust_ref[index] * (1.0 - table_ref[lax.bitwise_xor(me, index), 6])
        for index in range(platforms)
    ]

    def prepare(index, carry):
        block = blocks_ref[index]
        features = source_rows(block[0:3])
        stacked = jnp.concatenate(
            [features[:, part * quarter : (part + 1) * quarter] for part in range(QUARTERS)], axis=0
        )
        start = pl.multiple_of(index * quarter, quarter)
        rows_ref[pl.ds(start, quarter), :] = stacked.T.astype(BF16)
        strengths = strength_rows(block, scales).astype(BF16)
        for part in range(QUARTERS):
            weights_ref[part, :, pl.ds(start, quarter)] = strengths[
                :, part * quarter : (part + 1) * quarter
            ]
        return carry

    lax.fori_loop(0, blocks, prepare, 0)

    chunks = blocks * quarter // chunk
    steps = tiles * QUARTERS * chunks
    span = 256

    def distances(step, buffer):
        features = targets_ref[step // chunks]
        start = pl.multiple_of(step % chunks * chunk, chunk)
        for k in range(0, chunk, span):
            buffer[k : k + span, :] = jnp.dot(
                rows_ref[pl.ds(start + k, span), :], features, preferred_element_type=F32
            )

    def add_up(step, buffer):
        group = step // chunks
        start = pl.multiple_of(step % chunks * chunk, chunk)
        total = jnp.zeros((16, TILE), F32)
        for k in range(0, chunk, span):
            root = lax.rsqrt(buffer[k : k + span, :])
            pair = root * root * root
            high = pair.astype(BF16)
            low = (pair - high.astype(F32)).astype(BF16)
            weights = weights_ref[group % QUARTERS, :, pl.ds(start + k, span)]
            total = total + jnp.dot(weights, high, preferred_element_type=F32)
            total = total + jnp.dot(weights, low, preferred_element_type=F32)
        sums_ref[group // QUARTERS] += total

    distances(0, even_ref)

    def pairs(index, carry):
        step = 2 * index
        distances(step + 1, odd_ref)
        add_up(step, even_ref)
        distances(jnp.minimum(step + 2, steps - 1), even_ref)
        add_up(step + 1, odd_ref)
        return carry

    lax.fori_loop(0, steps // 2, pairs, 0)

    def velocity(tile):
        sums = sums_ref[tile]
        at = target_pos_ref[:, tile * TILE : (tile + 1) * TILE]
        a = [sums[c : c + 1] + sums[c + 3 : c + 4] for c in range(3)]
        b = [sums[c + 6 : c + 7] + sums[c + 9 : c + 10] + sums[c + 12 : c + 13] for c in range(3)]
        x = [at[c : c + 1] for c in range(3)]
        return [
            (a[1] * x[2] - a[2] * x[1] - b[0]) * inverse_four_pi,
            (a[2] * x[0] - a[0] * x[2] - b[1]) * inverse_four_pi,
            (a[0] * x[1] - a[1] * x[0] - b[2]) * inverse_four_pi,
        ]

    for tile in range(tiles - 1):
        induced_ref[:, tile * TILE : (tile + 1) * TILE] = jnp.concatenate(velocity(tile), axis=0)

    wind = [row[:, 0:LANES] for row in velocity(tiles - 1)]
    arm = [nodes[3 + c : 4 + c] for c in range(3)]
    turn = [table_ref[0, 9 + c] for c in range(3)]
    rigid = [
        table_ref[0, 6] + (turn[1] * arm[2] - turn[2] * arm[1]),
        table_ref[0, 7] + (turn[2] * arm[0] - turn[0] * arm[2]),
        table_ref[0, 8] + (turn[0] * arm[1] - turn[1] * arm[0]),
    ]
    relative = [1.0 + wind[0] - rigid[0], wind[1] - rigid[1], wind[2] - rigid[2]]
    magnitude = jnp.sqrt(
        relative[0] * relative[0] + relative[1] * relative[1] + relative[2] * relative[2]
    )
    force = [nodes[6:7] * magnitude * row for row in relative]
    moment = [
        arm[1] * force[2] - arm[2] * force[1],
        arm[2] * force[0] - arm[0] * force[2],
        arm[0] * force[1] - arm[1] * force[0],
    ]
    loads = [jnp.sum(row, axis=1, keepdims=True) for row in force + moment]

    lines = offset_ref.shape[1]
    segments = offset_ref.shape[2]

    def headings(number):
        which = lax.rem(number, 3)
        pick = lambda values: jnp.where(
            which == 0, values[0], jnp.where(which == 1, values[1], values[2])
        )
        return [pick(cosines), pick(sines), jnp.full(number.shape, 0.6, F32)]

    shape = (lines, segments)
    row_index = lax.broadcasted_iota(jnp.int32, shape, 0)
    node_index = lax.broadcasted_iota(jnp.int32, shape, 1)
    heading = headings(me * lines + row_index)
    depth = (segments - node_index).astype(F32)
    points = [-line_spacing * heading[c] * depth + offset_ref[c] for c in range(3)]
    fair = [jnp.zeros(shape, F32)] * 3
    for line in range(lines):
        owner = lax.bitwise_xor(me, line_platform_ref[line])
        fair = [jnp.where(row_index == line, table_ref[owner, c], fair[c]) for c in range(3)]
    last = node_index == segments - 1
    following = [
        jnp.where(last, fair[c], pltpu.roll(points[c], segments - 1, 1)) for c in range(3)
    ]

    def pulls(segment):
        length = jnp.sqrt(
            segment[0] * segment[0] + segment[1] * segment[1] + segment[2] * segment[2]
        )
        tension = line_stiffness * (length - rest_length) / rest_length
        return [tension / length * part for part in segment]

    pull = pulls([following[c] - points[c] for c in range(3)])
    for c in range(3):
        previous = jnp.where(node_index == 0, 0.0, pltpu.roll(pull[c], 1, 1))
        gravity = -node_weight if c == 2 else 0.0
        acceleration = pull[c] - previous + gravity - line_damping * line_velocity_ref[c]
        line_accel_ref[c] = jnp.where(node_index == 0, 0.0, acceleration)

    shape = (devices, LANES)
    sender = lax.bitwise_xor(lax.broadcasted_iota(jnp.int32, shape, 0), jnp.full(shape, me))
    number = lax.broadcasted_iota(jnp.int32, shape, 1)
    heading = headings(sender * lines + number)
    ends = [
        table_ref[0, c] - (-line_spacing * heading[c] + misc_ref[:, 9 + c, :]) for c in range(3)
    ]
    ours = jnp.logical_and(number < lines, misc_ref[:, 12, :] == me.astype(F32))
    pull = pulls(ends)
    for c in range(3):
        taken = jnp.where(ours, pull[c], 0.0)
        loads[c] = loads[c] - jnp.sum(jnp.sum(taken, axis=0, keepdims=True), axis=1, keepdims=True)

    history = history_ref[0]
    total = []
    for i in range(6):
        product = jnp.sum(memory_ref[i] * history, axis=0, keepdims=True)
        radiation = -jnp.sum(product, axis=1, keepdims=True)
        total.append(loads[i] + radiation - restoring_ref[i] * table_ref[0, i])
    for i in range(6):
        value = mass_ref[i, 0] * total[0]
        for j in range(1, 6):
            value = value + mass_ref[i, j] * total[j]
        accel_ref[i : i + 1, :] = value


def shards(
    particle_pos,
    vorticity,
    particle_owner,
    thrust_coef,
    node_pos,
    lever_arm,
    chord_coef,
    node_platform,
    platform_pos,
    platform_vel,
    velocity_history,
    memory_kernel,
    restoring,
    inverse_mass,
    line_offset,
    line_velocity,
    line_platform,
):
    devices = lax.axis_size("blk")
    me = lax.axis_index("blk")
    own_count = particle_pos.shape[1]
    lines, segments = line_offset.shape[1:]

    def wide(rows):
        return jnp.pad(rows, ((0, 0), (0, LANES - rows.shape[1])))

    motion = jnp.concatenate([platform_pos, platform_vel], axis=0).reshape(1, 12)
    misc = jnp.concatenate(
        [
            node_pos,
            lever_arm,
            chord_coef[None],
            node_platform.astype(F32)[None],
            wide(motion),
            wide(line_offset[:, :, segments - 1]),
            wide(line_platform.astype(F32)[None]),
            jnp.zeros((3, LANES), F32),
        ],
        axis=0,
    )[None]
    own = jnp.concatenate(
        [
            particle_pos,
            vorticity,
            particle_owner.astype(F32)[None],
            jnp.zeros((1, own_count), F32),
        ],
        axis=0,
    )[None]

    def swap(values, distance):
        return lax.ppermute(values, "blk", [(i, i ^ distance) for i in range(devices)])

    distance = 1
    while distance < devices:
        misc = jnp.concatenate([misc, swap(misc, distance)], axis=0)
        distance *= 2
    received = [own] + [swap(own, distance) for distance in range(2, devices, 2)]
    half = jnp.concatenate(received, axis=0)
    blocks = jnp.concatenate([half, swap(half, 1)], axis=0)

    table = misc[:, 8, 0:16]
    tiles = own_count // TILE + 1
    rows = devices * own_count // QUARTERS
    chunk = min(rows, 4096)
    smem = pl.BlockSpec(memory_space=pltpu.SMEM)
    vmem = pl.BlockSpec(memory_space=pltpu.VMEM)
    return pl.pallas_call(
        functools.partial(step_kernel, chunk),
        in_specs=[smem] * 6 + [vmem] * 7,
        out_specs=(vmem,) * 3,
        out_shape=(
            jax.ShapeDtypeStruct(particle_pos.shape, F32),
            jax.ShapeDtypeStruct(platform_pos.shape, F32),
            jax.ShapeDtypeStruct(line_offset.shape, F32),
        ),
        scratch_shapes=[
            pltpu.VMEM((rows, LANES), BF16),
            pltpu.VMEM((QUARTERS, 16, rows), BF16),
            pltpu.VMEM((tiles * QUARTERS, LANES, TILE), BF16),
            pltpu.VMEM((3, tiles * TILE), F32),
            pltpu.VMEM((chunk, TILE), F32),
            pltpu.VMEM((chunk, TILE), F32),
            pltpu.VMEM((tiles, 16, TILE), F32),
        ],
        compiler_params=pltpu.CompilerParams(vmem_limit_bytes=56 * 2**20),
        name="coupled_step",
    )(
        me.astype(jnp.int32)[None],
        table,
        thrust_coef,
        restoring,
        inverse_mass,
        line_platform,
        misc,
        particle_pos,
        blocks,
        velocity_history,
        memory_kernel,
        line_offset,
        line_velocity,
    )


def solution(mesh):
    return jax.shard_map(
        shards,
        mesh=mesh,
        in_specs=(
            P(None, ("farm", "blk")),
            P(None, ("farm", "blk")),
            P(("farm", "blk")),
            P("farm"),
            P(None, ("farm", "blk")),
            P(None, ("farm", "blk")),
            P(("farm", "blk")),
            P(("farm", "blk")),
            P(None, ("farm", "blk")),
            P(None, ("farm", "blk")),
            P(("farm", "blk"), None, None),
            P(),
            P(),
            P(),
            P(None, ("farm", "blk"), None),
            P(None, ("farm", "blk"), None),
            P(("farm", "blk")),
        ),
        out_specs=(
            P(None, ("farm", "blk")),
            P(None, ("farm", "blk")),
            P(None, ("farm", "blk"), None),
        ),
        check_vma=False,
    )
```

```python
import functools
import math

import jax
import jax.numpy as jnp
import numpy as np
from jax import lax
from jax.experimental import pallas as pl
from jax.experimental.pallas import tpu as pltpu
from jax.sharding import PartitionSpec as P

core_square = 0.01
inverse_four_pi = 0.25 / math.pi
line_spacing = 1.0
rest_length = 0.95 * math.sqrt(1.36)
line_stiffness = 20.0
node_weight = 0.5
line_damping = 0.5
F32 = jnp.float32
BF16 = jnp.bfloat16
LANES = 128
TILE = 256
QUARTERS = 4
FEATURES = 32
SPAN = 256
third_turn = np.float32(2.0 * math.pi / 3.0)
cosines = [float(np.cos(third_turn * np.float32(k))) for k in range(3)]
sines = [float(np.sin(third_turn * np.float32(k))) for k in range(3)]


def piece(values):
    return values.astype(BF16).astype(F32)


def coordinate_pieces(pos, extra):
    first = jnp.round(pos * 64.0) * (1.0 / 64.0)
    rest = pos - first
    second = jnp.round(rest * 16384.0) * (1.0 / 16384.0)
    third = piece(rest - second)
    square = first * first
    norm = square[0:1] + square[1:2] + square[2:3]
    cross = rest * (pos + first)
    small = cross[0:1] + cross[1:2] + cross[2:3] + extra
    norm_a = piece(norm)
    norm_b = norm - norm_a
    small_a = piece(small)
    small_b = small - small_a
    return first, second, third, norm_a, norm_b, small_a, small_b


def source_rows(pos):
    first, second, third, norm_a, norm_b, small_a, small_b = coordinate_pieces(pos, 0.0)
    one = jnp.ones_like(norm_a)
    return jnp.concatenate(
        [first, norm_a, one, norm_b, one, small_a, one, first, second, small_b, one]
        + [second, first, third, second, third],
        axis=0,
    )


def target_rows(pos):
    first, second, third, norm_a, norm_b, small_a, small_b = coordinate_pieces(pos, core_square)
    one = jnp.ones_like(norm_a)
    first, second, third = -2.0 * first, -2.0 * second, -2.0 * third
    return jnp.concatenate(
        [first, one, norm_a, one, norm_b, one, small_a, second, first, one, small_b]
        + [second, third, first, third, second],
        axis=0,
    )


def strength_rows(block, scales):
    pos, vorticity, owner = block[0:3], block[3:6], block[6:7]
    scale = jnp.zeros_like(owner)
    for index, value in enumerate(scales):
        scale = jnp.where(owner == float(index), value, scale)
    strength = vorticity * scale
    s_hi = piece(strength)
    s_lo = piece(strength - s_hi)
    held = s_hi + s_lo
    moment = jnp.concatenate(
        [
            held[1:2] * pos[2:3] - held[2:3] * pos[1:2],
            held[2:3] * pos[0:1] - held[0:1] * pos[2:3],
            held[0:1] * pos[1:2] - held[1:2] * pos[0:1],
        ],
        axis=0,
    )
    m_hi = piece(moment)
    m_mid = piece(moment - m_hi)
    m_lo = moment - m_hi - m_mid
    return jnp.concatenate([s_hi, s_lo, m_hi, m_mid, m_lo, jnp.zeros_like(owner)], axis=0)


def strength_scales(me, table_ref, thrust_ref):
    return [
        thrust_ref[index] * (1.0 - table_ref[lax.bitwise_xor(me, index), 6])
        for index in range(thrust_ref.shape[0])
    ]


def pair_sums(block_refs, scales, target_pos_ref, sums_ref, scratch):
    rows_ref, weights_ref, targets_ref, even_ref, odd_ref = scratch
    quarter = block_refs[0].shape[2] // QUARTERS
    tiles = sums_ref.shape[0]
    for tile in range(tiles):
        features = target_rows(target_pos_ref[:, tile * TILE : (tile + 1) * TILE]).astype(BF16)
        for part in range(QUARTERS):
            slot = targets_ref.at[tile * QUARTERS + part]
            slot[...] = jnp.zeros((LANES, TILE), BF16)
            slot[part * FEATURES : (part + 1) * FEATURES, :] = features

    first = 0
    for block_ref in block_refs:

        def prepare(index, carry, block_ref=block_ref, first=first):
            block = block_ref[index]
            features = source_rows(block[0:3])
            stacked = jnp.concatenate(
                [features[:, part * quarter : (part + 1) * quarter] for part in range(QUARTERS)],
                axis=0,
            )
            start = pl.multiple_of((first + index) * quarter, quarter)
            rows_ref[pl.ds(start, quarter), :] = stacked.T.astype(BF16)
            strengths = strength_rows(block, scales).astype(BF16)
            for part in range(QUARTERS):
                weights_ref[part, :, pl.ds(start, quarter)] = strengths[
                    :, part * quarter : (part + 1) * quarter
                ]
            return carry

        lax.fori_loop(0, block_ref.shape[0], prepare, 0)
        first += block_ref.shape[0]

    reach = even_ref.shape[0] // QUARTERS
    chunks = rows_ref.shape[0] // reach
    steps = tiles * chunks
    span = min(SPAN, reach)

    def distances(step, buffer):
        tile = step // chunks
        start = pl.multiple_of(step % chunks * reach, reach)
        for part in range(QUARTERS):
            features = targets_ref[tile * QUARTERS + part]
            for k in range(0, reach, span):
                at = part * reach + k
                buffer[at : at + span, :] = jnp.dot(
                    rows_ref[pl.ds(start + k, span), :], features, preferred_element_type=F32
                )

    def add_up(step, buffer):
        tile = step // chunks
        start = pl.multiple_of(step % chunks * reach, reach)
        total = jnp.zeros((16, TILE), F32)
        for part in range(QUARTERS):
            for k in range(0, reach, span):
                at = part * reach + k
                root = lax.rsqrt(buffer[at : at + span, :])
                pair = root * root * root
                high = pair.astype(BF16)
                low = (pair - high.astype(F32)).astype(BF16)
                weights = weights_ref[part, :, pl.ds(start + k, span)]
                total = total + jnp.dot(weights, high, preferred_element_type=F32)
                total = total + jnp.dot(weights, low, preferred_element_type=F32)
        sums_ref[tile] += total

    def two_steps(index, carry):
        step = 2 * index
        distances(step + 1, odd_ref)
        add_up(step, even_ref)
        distances(step + 2, even_ref)
        add_up(step + 1, odd_ref)
        return carry

    distances(0, even_ref)
    doubles = (steps - 1) // 2
    lax.fori_loop(0, doubles, two_steps, 0)
    if steps % 2 == 0:
        distances(steps - 1, odd_ref)
        add_up(steps - 2, even_ref)
        add_up(steps - 1, odd_ref)
    else:
        add_up(steps - 1, even_ref)


def platform_nodes(me, misc_ref):
    devices = misc_ref.shape[0]
    on_platform = misc_ref[:, 7, :] == me.astype(F32)
    mark = on_platform.astype(F32)
    upper = lax.broadcasted_iota(jnp.int32, (LANES, LANES), 0) <= lax.broadcasted_iota(
        jnp.int32, (LANES, LANES), 1
    )
    counted = jnp.dot(mark.astype(BF16), upper.astype(F32).astype(BF16), preferred_element_type=F32)
    below = lax.broadcasted_iota(jnp.int32, (devices, devices), 0) > lax.broadcasted_iota(
        jnp.int32, (devices, devices), 1
    )
    totals = jnp.broadcast_to(counted[:, LANES - 1 :], counted.shape)
    before = jnp.dot(below.astype(F32).astype(BF16), totals.astype(BF16), preferred_element_type=F32)
    rank = jnp.where(on_platform, counted - 1.0 + before, -1.0)
    slots = lax.broadcasted_iota(jnp.int32, (LANES, LANES), 0).astype(F32)
    picked = jnp.zeros((24, LANES), F32)
    for device in range(devices):
        data = misc_ref[device, 0:8, :]
        hi = piece(data)
        mid = piece(data - hi)
        pieces = jnp.concatenate([hi, mid, data - hi - mid], axis=0).astype(BF16)
        pick = (slots == rank[device : device + 1]).astype(F32).astype(BF16)
        picked = picked + lax.dot_general(
            pieces, pick, (((1,), (1,)), ((), ())), preferred_element_type=F32
        )
    return picked[0:8] + picked[8:16] + picked[16:24]


def headings(number):
    which = lax.rem(number, 3)
    pick = lambda values: jnp.where(
        which == 0, values[0], jnp.where(which == 1, values[1], values[2])
    )
    return [pick(cosines), pick(sines), jnp.full(number.shape, 0.6, F32)]


def pulls(segment):
    length = jnp.sqrt(segment[0] * segment[0] + segment[1] * segment[1] + segment[2] * segment[2])
    tension = line_stiffness * (length - rest_length) / rest_length
    return [tension / length * part for part in segment]


def own_lines(me, table_ref, line_platform_ref, offset_ref, line_velocity_ref, line_accel_ref):
    lines, segments = offset_ref.shape[1:]
    shape = (lines, segments)
    row_index = lax.broadcasted_iota(jnp.int32, shape, 0)
    node_index = lax.broadcasted_iota(jnp.int32, shape, 1)
    heading = headings(me * lines + row_index)
    depth = (segments - node_index).astype(F32)
    points = [-line_spacing * heading[c] * depth + offset_ref[c] for c in range(3)]
    fair = [jnp.zeros(shape, F32)] * 3
    for line in range(lines):
        owner = lax.bitwise_xor(me, line_platform_ref[line])
        fair = [jnp.where(row_index == line, table_ref[owner, c], fair[c]) for c in range(3)]
    last = node_index == segments - 1
    following = [
        jnp.where(last, fair[c], pltpu.roll(points[c], segments - 1, 1)) for c in range(3)
    ]
    pull = pulls([following[c] - points[c] for c in range(3)])
    for c in range(3):
        previous = jnp.where(node_index == 0, 0.0, pltpu.roll(pull[c], 1, 1))
        gravity = -node_weight if c == 2 else 0.0
        acceleration = pull[c] - previous + gravity - line_damping * line_velocity_ref[c]
        line_accel_ref[c] = jnp.where(node_index == 0, 0.0, acceleration)


def platform_pulls(me, table_ref, misc_ref, lines):
    shape = (misc_ref.shape[0], LANES)
    sender = lax.bitwise_xor(lax.broadcasted_iota(jnp.int32, shape, 0), jnp.full(shape, me))
    number = lax.broadcasted_iota(jnp.int32, shape, 1)
    heading = headings(sender * lines + number)
    ends = [
        table_ref[0, c] - (-line_spacing * heading[c] + misc_ref[:, 9 + c, :]) for c in range(3)
    ]
    ours = jnp.logical_and(number < lines, misc_ref[:, 12, :] == me.astype(F32))
    taken = [jnp.where(ours, part, 0.0) for part in pulls(ends)]
    return [jnp.sum(jnp.sum(t, axis=0, keepdims=True), axis=1, keepdims=True) for t in taken]


def first_kernel(
    me_ref,
    table_ref,
    thrust_ref,
    restoring_ref,
    line_platform_ref,
    misc_ref,
    pos_ref,
    history_ref,
    memory_ref,
    offset_ref,
    line_velocity_ref,
    block_ref,
    target_pos_ref,
    state_ref,
    line_accel_ref,
    sums_ref,
    *scratch,
):
    me = me_ref[0]
    own_count = pos_ref.shape[1]
    nodes = platform_nodes(me, misc_ref)
    current = jnp.concatenate([nodes[c : c + 1] + table_ref[0, c] for c in range(3)], axis=0)
    target_pos_ref[:, 0:own_count] = pos_ref[...]
    target_pos_ref[:, own_count : own_count + LANES] = current
    target_pos_ref[:, own_count + LANES :] = current
    sums_ref[...] = jnp.zeros_like(sums_ref)
    own_lines(me, table_ref, line_platform_ref, offset_ref, line_velocity_ref, line_accel_ref)
    pull = platform_pulls(me, table_ref, misc_ref, offset_ref.shape[1])
    history = jnp.concatenate([history_ref[j] for j in range(6)], axis=0)
    state_ref[0:8, :] = nodes
    for i in range(6):
        product = jnp.sum(memory_ref[i] * history, axis=0, keepdims=True)
        value = -jnp.sum(product, axis=1, keepdims=True) - restoring_ref[i] * table_ref[0, i]
        if i < 3:
            value = value - pull[i]
        state_ref[8 + i : 9 + i, :] = jnp.broadcast_to(value, (1, LANES))
    scales = strength_scales(me, table_ref, thrust_ref)
    pair_sums([block_ref], scales, target_pos_ref, sums_ref, scratch)


def middle_kernel(count, me_ref, table_ref, thrust_ref, target_pos_ref, before_ref, *rest):
    block_refs, (sums_ref, *scratch) = rest[:count], rest[count:]
    sums_ref[...] = before_ref[...]
    scales = strength_scales(me_ref[0], table_ref, thrust_ref)
    pair_sums(block_refs, scales, target_pos_ref, sums_ref, scratch)


def last_kernel(
    count, me_ref, table_ref, thrust_ref, mass_ref, target_pos_ref, before_ref, state_ref, *rest
):
    block_refs, (induced_ref, accel_ref, sums_ref, *scratch) = rest[:count], rest[count:]
    sums_ref[...] = before_ref[...]
    scales = strength_scales(me_ref[0], table_ref, thrust_ref)
    pair_sums(block_refs, scales, target_pos_ref, sums_ref, scratch)
    tiles = sums_ref.shape[0]

    def velocity(tile):
        sums = sums_ref[tile]
        at = target_pos_ref[:, tile * TILE : (tile + 1) * TILE]
        a = [sums[c : c + 1] + sums[c + 3 : c + 4] for c in range(3)]
        b = [sums[c + 6 : c + 7] + sums[c + 9 : c + 10] + sums[c + 12 : c + 13] for c in range(3)]
        x = [at[c : c + 1] for c in range(3)]
        return [
            (a[1] * x[2] - a[2] * x[1] - b[0]) * inverse_four_pi,
            (a[2] * x[0] - a[0] * x[2] - b[1]) * inverse_four_pi,
            (a[0] * x[1] - a[1] * x[0] - b[2]) * inverse_four_pi,
        ]

    for tile in range(tiles - 1):
        induced_ref[:, tile * TILE : (tile + 1) * TILE] = jnp.concatenate(velocity(tile), axis=0)

    wind = [row[:, 0:LANES] for row in velocity(tiles - 1)]
    arm = [state_ref[3 + c : 4 + c, :] for c in range(3)]
    turn = [table_ref[0, 9 + c] for c in range(3)]
    rigid = [
        table_ref[0, 6] + (turn[1] * arm[2] - turn[2] * arm[1]),
        table_ref[0, 7] + (turn[2] * arm[0] - turn[0] * arm[2]),
        table_ref[0, 8] + (turn[0] * arm[1] - turn[1] * arm[0]),
    ]
    relative = [1.0 + wind[0] - rigid[0], wind[1] - rigid[1], wind[2] - rigid[2]]
    magnitude = jnp.sqrt(
        relative[0] * relative[0] + relative[1] * relative[1] + relative[2] * relative[2]
    )
    force = [state_ref[6:7, :] * magnitude * row for row in relative]
    moment = [
        arm[1] * force[2] - arm[2] * force[1],
        arm[2] * force[0] - arm[0] * force[2],
        arm[0] * force[1] - arm[1] * force[0],
    ]
    total = [
        jnp.sum(row, axis=1, keepdims=True) + state_ref[8 + i : 9 + i, 0:1]
        for i, row in enumerate(force + moment)
    ]
    lane = lax.broadcasted_iota(jnp.int32, (1, LANES), 1)
    result = jnp.zeros((1, LANES), F32)
    for i in range(6):
        value = mass_ref[i, 0] * total[0]
        for j in range(1, 6):
            value = value + mass_ref[i, j] * total[j]
        result = jnp.where(lane == i, value, result)
    accel_ref[...] = result[:, 0:6]


def shards(
    particle_pos,
    vorticity,
    particle_owner,
    thrust_coef,
    node_pos,
    lever_arm,
    chord_coef,
    node_platform,
    platform_pos,
    platform_vel,
    velocity_history,
    memory_kernel,
    restoring,
    inverse_mass,
    line_offset,
    line_velocity,
    line_platform,
):
    devices = lax.axis_size("blk")
    me = lax.axis_index("blk")
    own_count = particle_pos.shape[1]
    segments = line_offset.shape[2]
    tiles = own_count // TILE + 1

    def wide(rows):
        return jnp.pad(rows, ((0, 0), (0, LANES - rows.shape[1])))

    motion = jnp.concatenate([platform_pos, platform_vel], axis=0).reshape(1, 12)
    misc = jnp.concatenate(
        [
            node_pos,
            lever_arm,
            chord_coef[None],
            node_platform.astype(F32)[None],
            wide(motion),
            wide(line_offset[:, :, segments - 1]),
            wide(line_platform.astype(F32)[None]),
            jnp.zeros((3, LANES), F32),
        ],
        axis=0,
    )[None]
    own = jnp.concatenate(
        [
            particle_pos,
            vorticity,
            particle_owner.astype(F32)[None],
            jnp.zeros((1, own_count), F32),
        ],
        axis=0,
    )[None]

    def swap(values, distance):
        return lax.ppermute(values, "blk", [(i, i ^ distance) for i in range(devices)])

    distance = 1
    while distance < devices:
        misc = jnp.concatenate([misc, swap(misc, distance)], axis=0)
        distance *= 2
    table = misc[:, 8, 0:16]

    near = [swap(own, 1), swap(own, 2)]
    near.append(swap(near[1], 1))
    direct = []
    if devices > 4:
        direct.append(jnp.concatenate([swap(own, 4), swap(own, 6)], axis=0))

    smem = pl.BlockSpec(memory_space=pltpu.SMEM)
    vmem = pl.BlockSpec(memory_space=pltpu.VMEM)
    sums_shape = jax.ShapeDtypeStruct((tiles, 16, TILE), F32)

    def call(kernel, scalars, arrays, blocks, out_shape):
        count = sum(block.shape[0] for block in blocks)
        rows = count * own_count // QUARTERS
        reach = next(r for r in (1024, 512) if rows % r == 0)
        work = count * own_count * tiles * TILE
        return pl.pallas_call(
            kernel,
            in_specs=[smem] * len(scalars) + [vmem] * (len(arrays) + len(blocks)),
            out_specs=(vmem,) * len(out_shape),
            out_shape=out_shape,
            scratch_shapes=[
                pltpu.VMEM((rows, LANES), BF16),
                pltpu.VMEM((QUARTERS, 16, rows), BF16),
                pltpu.VMEM((tiles * QUARTERS, LANES, TILE), BF16),
                pltpu.VMEM((QUARTERS * reach, TILE), F32),
                pltpu.VMEM((QUARTERS * reach, TILE), F32),
            ],
            compiler_params=pltpu.CompilerParams(vmem_limit_bytes=48 * 2**20),
            cost_estimate=pl.CostEstimate(
                flops=1200 * work, bytes_accessed=count * own_count * 32, transcendentals=0
            ),
            name="pairs",
        )(*scalars, *arrays, *blocks)

    me = me.astype(jnp.int32)[None]
    target_pos, state, line_accel, sums = call(
        first_kernel,
        [me, table, thrust_coef, restoring, line_platform],
        [misc, particle_pos, jnp.transpose(velocity_history, (1, 0, 2)), memory_kernel]
        + [line_offset, line_velocity],
        [own],
        (
            jax.ShapeDtypeStruct((3, tiles * TILE), F32),
            jax.ShapeDtypeStruct((16, LANES), F32),
            jax.ShapeDtypeStruct(line_offset.shape, F32),
            sums_shape,
        ),
    )
    groups = [near]
    distance = 4
    while len(groups) < 2 or distance < devices:
        own, sums, *direct = lax.optimization_barrier((own, sums, *direct))
        if distance < devices:
            groups.append([direct[-1], swap(direct[-1], 1)])
        distance *= 2
        if distance < devices:
            sent = [swap(own, d) for d in range(distance, 2 * distance, 2)]
            direct.append(jnp.concatenate(sent, axis=0))
        if len(groups) < 2:
            break
        blocks = groups.pop(0)
        (sums,) = call(
            functools.partial(middle_kernel, len(blocks)),
            [me, table, thrust_coef],
            [target_pos, sums],
            blocks,
            (sums_shape,),
        )
    blocks = groups[-1]
    induced, accel, unused = call(
        functools.partial(last_kernel, len(blocks)),
        [me, table, thrust_coef, inverse_mass],
        [target_pos, sums, state],
        blocks,
        (
            jax.ShapeDtypeStruct(particle_pos.shape, F32),
            jax.ShapeDtypeStruct((1, 6), F32),
            sums_shape,
        ),
    )
    return (induced, accel.reshape(6, 1), line_accel)


def solution(mesh):
    return jax.shard_map(
        shards,
        mesh=mesh,
        in_specs=(
            P(None, ("farm", "blk")),
            P(None, ("farm", "blk")),
            P(("farm", "blk")),
            P("farm"),
            P(None, ("farm", "blk")),
            P(None, ("farm", "blk")),
            P(("farm", "blk")),
            P(("farm", "blk")),
            P(None, ("farm", "blk")),
            P(None, ("farm", "blk")),
            P(("farm", "blk"), None, None),
            P(),
            P(),
            P(),
            P(None, ("farm", "blk"), None),
            P(None, ("farm", "blk"), None),
            P(("farm", "blk")),
        ),
        out_specs=(
            P(None, ("farm", "blk")),
            P(None, ("farm", "blk")),
            P(None, ("farm", "blk"), None),
        ),
        check_vma=False,
    )
```

```python
import functools
import math

import jax
import jax.numpy as jnp
import numpy as np
from jax import lax
from jax.experimental import pallas as pl
from jax.experimental.pallas import tpu as pltpu
from jax.sharding import PartitionSpec as P

core_square = 0.01
inverse_four_pi = 0.25 / math.pi
line_spacing = 1.0
rest_length = 0.95 * math.sqrt(1.36)
line_stiffness = 20.0
node_weight = 0.5
line_damping = 0.5
F32 = jnp.float32
BF16 = jnp.bfloat16
LANES = 128
TILE = 256
QUARTERS = 4
FEATURES = 32
SPAN = 256
third_turn = np.float32(2.0 * math.pi / 3.0)
cosines = [float(np.cos(third_turn * np.float32(k))) for k in range(3)]
sines = [float(np.sin(third_turn * np.float32(k))) for k in range(3)]


def piece(values):
    return values.astype(BF16).astype(F32)


def coordinate_pieces(pos, extra):
    first = jnp.round(pos * 64.0) * (1.0 / 64.0)
    rest = pos - first
    second = jnp.round(rest * 16384.0) * (1.0 / 16384.0)
    third = piece(rest - second)
    square = first * first
    norm = square[0:1] + square[1:2] + square[2:3]
    cross = rest * (pos + first)
    small = cross[0:1] + cross[1:2] + cross[2:3] + extra
    norm_a = piece(norm)
    norm_b = norm - norm_a
    small_a = piece(small)
    small_b = small - small_a
    return first, second, third, norm_a, norm_b, small_a, small_b


def source_rows(pos):
    first, second, third, norm_a, norm_b, small_a, small_b = coordinate_pieces(pos, 0.0)
    one = jnp.ones_like(norm_a)
    return jnp.concatenate(
        [first, norm_a, one, norm_b, one, small_a, one, first, second, small_b, one]
        + [second, first, third, second, third],
        axis=0,
    )


def target_rows(pos):
    first, second, third, norm_a, norm_b, small_a, small_b = coordinate_pieces(pos, core_square)
    one = jnp.ones_like(norm_a)
    first, second, third = -2.0 * first, -2.0 * second, -2.0 * third
    return jnp.concatenate(
        [first, one, norm_a, one, norm_b, one, small_a, second, first, one, small_b]
        + [second, third, first, third, second],
        axis=0,
    )


def strength_rows(block, scales):
    pos, vorticity, owner = block[0:3], block[3:6], block[6:7]
    scale = jnp.zeros_like(owner)
    for index, value in enumerate(scales):
        scale = jnp.where(owner == float(index), value, scale)
    strength = vorticity * scale
    s_hi = piece(strength)
    s_lo = piece(strength - s_hi)
    held = s_hi + s_lo
    moment = jnp.concatenate(
        [
            held[1:2] * pos[2:3] - held[2:3] * pos[1:2],
            held[2:3] * pos[0:1] - held[0:1] * pos[2:3],
            held[0:1] * pos[1:2] - held[1:2] * pos[0:1],
        ],
        axis=0,
    )
    m_hi = piece(moment)
    m_mid = piece(moment - m_hi)
    m_lo = moment - m_hi - m_mid
    return jnp.concatenate([s_hi, s_lo, m_hi, m_mid, m_lo, jnp.zeros_like(owner)], axis=0)


def strength_scales(me, table_ref, thrust_ref):
    return [
        thrust_ref[index] * (1.0 - table_ref[lax.bitwise_xor(me, index), 6])
        for index in range(thrust_ref.shape[0])
    ]


def pair_sums(block_refs, scales, target_pos_ref, sums_ref, scratch):
    rows_ref, weights_ref, targets_ref, even_ref, odd_ref = scratch
    quarter = block_refs[0].shape[2] // QUARTERS
    tiles = sums_ref.shape[0] - 1
    halves = QUARTERS // 2
    for tile in range(tiles):
        features = target_rows(target_pos_ref[:, tile * TILE : (tile + 1) * TILE]).astype(BF16)
        for part in range(QUARTERS):
            slot = targets_ref.at[tile * QUARTERS + part]
            slot[...] = jnp.zeros((LANES, TILE), BF16)
            slot[part * FEATURES : (part + 1) * FEATURES, :] = features
    features = target_rows(target_pos_ref[:, tiles * TILE : (tiles + 1) * TILE]).astype(BF16)
    left = features[:, 0:LANES]
    for half in range(halves):
        slot = targets_ref.at[tiles * QUARTERS + half]
        slot[...] = jnp.zeros((LANES, TILE), BF16)
        for side in range(2):
            part = 2 * half + side
            slot[part * FEATURES : (part + 1) * FEATURES, side * LANES : (side + 1) * LANES] = left

    first = 0
    for block_ref in block_refs:

        def prepare(index, carry, block_ref=block_ref, first=first):
            block = block_ref[index]
            features = source_rows(block[0:3])
            stacked = jnp.concatenate(
                [features[:, part * quarter : (part + 1) * quarter] for part in range(QUARTERS)],
                axis=0,
            )
            start = pl.multiple_of((first + index) * quarter, quarter)
            rows_ref[pl.ds(start, quarter), :] = stacked.T.astype(BF16)
            strengths = strength_rows(block, scales).astype(BF16)
            for part in range(QUARTERS):
                weights_ref[part, :, pl.ds(start, quarter)] = strengths[
                    :, part * quarter : (part + 1) * quarter
                ]
            return carry

        lax.fori_loop(0, block_ref.shape[0], prepare, 0, unroll=4)
        first += block_ref.shape[0]

    rows = rows_ref.shape[0]
    reach = even_ref.shape[0] // QUARTERS
    chunks = rows // reach
    steps = tiles * chunks
    span = SPAN

    def distances_into(buffer, at, start, count, features):
        for k in range(0, count, span):
            buffer[at + k : at + k + span, :] = jnp.dot(
                rows_ref[pl.ds(start + k, span), :], features, preferred_element_type=F32
            )

    def summed(buffer, at, weights):
        root = lax.rsqrt(buffer[at : at + span, :])
        pair = root * root * root
        high = pair.astype(BF16)
        low = (pair - high.astype(F32)).astype(BF16)
        return jnp.dot(weights, high, preferred_element_type=F32) + jnp.dot(
            weights, low, preferred_element_type=F32
        )

    def distances(step, buffer):
        tile = step // chunks
        start = pl.multiple_of(step % chunks * reach, reach)
        for part in range(QUARTERS):
            features = targets_ref[tile * QUARTERS + part]
            distances_into(buffer, part * reach, start, reach, features)

    def add_up(step, buffer):
        tile = step // chunks
        start = pl.multiple_of(step % chunks * reach, reach)
        total = jnp.zeros((16, TILE), F32)
        for part in range(QUARTERS):
            for k in range(0, reach, span):
                weights = weights_ref[part, :, pl.ds(start + k, span)]
                total = total + summed(buffer, part * reach + k, weights)
        sums_ref[tile] += total

    node_reach = min(rows, 2 * reach)

    def node_distances(start, buffer):
        for half in range(halves):
            features = targets_ref[tiles * QUARTERS + half]
            distances_into(buffer, half * node_reach, start, node_reach, features)

    def node_add_up(start, buffer):
        total = jnp.zeros((32, TILE), F32)
        for half in range(halves):
            for k in range(0, node_reach, span):
                weights = weights_ref[2 * half : 2 * half + 2, :, pl.ds(start + k, span)]
                weights = weights.reshape(32, span)
                total = total + summed(buffer, half * node_reach + k, weights)
        sums_ref[tiles, :, 0:LANES] += total[0:16, 0:LANES] + total[16:32, LANES:]

    def two_steps(index, carry):
        step = 2 * index
        distances(step + 1, odd_ref)
        add_up(step, even_ref)
        distances(step + 2, even_ref)
        add_up(step + 1, odd_ref)
        return carry

    distances(0, even_ref)
    doubles = (steps - 1) // 2
    lax.fori_loop(0, doubles, two_steps, 0)
    stages = [(functools.partial(distances, k), functools.partial(add_up, k)) for k in range(2 * doubles, steps)]
    stages += [
        (functools.partial(node_distances, start), functools.partial(node_add_up, start))
        for start in range(0, rows, node_reach)
    ]
    buffers = [even_ref, odd_ref]
    for index, (unused, add) in enumerate(stages):
        if index + 1 < len(stages):
            stages[index + 1][0](buffers[(index + 1) % 2])
        add(buffers[index % 2])


def misc_row(misc_ref, row):
    return misc_ref[:, row * LANES : (row + 1) * LANES]


def pack_kernel(
    line_platform_ref,
    pos_ref,
    vorticity_ref,
    owner_ref,
    node_pos_ref,
    lever_arm_ref,
    chord_ref,
    node_platform_ref,
    platform_pos_ref,
    platform_vel_ref,
    offset_ref,
    own_ref,
):
    own_ref[0, 0:3, :] = pos_ref[...]
    own_ref[0, 3:6, :] = vorticity_ref[...]
    own_ref[0, 6:7, :] = owner_ref[...].astype(F32)
    own_ref[0, 7:8, :] = jnp.zeros(owner_ref.shape, F32)

    def put(row, values):
        own_ref[0, 7:8, row * LANES : row * LANES + values.shape[1]] = values

    lane = lax.broadcasted_iota(jnp.int32, (1, LANES), 1)
    for c in range(3):
        put(c, node_pos_ref[c : c + 1, :])
        put(3 + c, lever_arm_ref[c : c + 1, :])
        row = jnp.zeros((1, LANES), F32)
        for line in range(offset_ref.shape[1]):
            row = jnp.where(lane == line, offset_ref[c, line : line + 1, LANES - 1 :], row)
        put(9 + c, row)
    put(6, chord_ref[...])
    put(7, node_platform_ref[...].astype(F32))
    put(8, jnp.concatenate([platform_pos_ref[...], platform_vel_ref[...]], axis=1))
    row = jnp.zeros((1, LANES), F32)
    for line in range(offset_ref.shape[1]):
        row = jnp.where(lane == line, line_platform_ref[line].astype(F32), row)
    put(12, row)


def platform_nodes(me, misc_ref):
    devices = misc_ref.shape[0]
    on_platform = misc_row(misc_ref, 7) == me.astype(F32)
    mark = on_platform.astype(F32)
    upper = lax.broadcasted_iota(jnp.int32, (LANES, LANES), 0) <= lax.broadcasted_iota(
        jnp.int32, (LANES, LANES), 1
    )
    counted = jnp.dot(mark.astype(BF16), upper.astype(F32).astype(BF16), preferred_element_type=F32)
    below = lax.broadcasted_iota(jnp.int32, (devices, devices), 0) > lax.broadcasted_iota(
        jnp.int32, (devices, devices), 1
    )
    totals = jnp.broadcast_to(counted[:, LANES - 1 :], counted.shape)
    before = jnp.dot(below.astype(F32).astype(BF16), totals.astype(BF16), preferred_element_type=F32)
    rank = jnp.where(on_platform, counted - 1.0 + before, -1.0)
    slots = lax.broadcasted_iota(jnp.int32, (LANES, LANES), 0).astype(F32)
    picked = jnp.zeros((24, LANES), F32)
    for device in range(devices):
        data = jnp.concatenate(
            [misc_ref[device : device + 1, k * LANES : (k + 1) * LANES] for k in range(8)], axis=0
        )
        hi = piece(data)
        mid = piece(data - hi)
        pieces = jnp.concatenate([hi, mid, data - hi - mid], axis=0).astype(BF16)
        pick = (slots == rank[device : device + 1]).astype(F32).astype(BF16)
        picked = picked + lax.dot_general(
            pieces, pick, (((1,), (1,)), ((), ())), preferred_element_type=F32
        )
    return picked[0:8] + picked[8:16] + picked[16:24]


def headings(number):
    which = lax.rem(number, 3)
    pick = lambda values: jnp.where(
        which == 0, values[0], jnp.where(which == 1, values[1], values[2])
    )
    return [pick(cosines), pick(sines), jnp.full(number.shape, 0.6, F32)]


def pulls(segment):
    length = jnp.sqrt(segment[0] * segment[0] + segment[1] * segment[1] + segment[2] * segment[2])
    tension = line_stiffness * (length - rest_length) / rest_length
    return [tension / length * part for part in segment]


def own_lines(me, table_ref, line_platform_ref, offset_ref, line_velocity_ref, line_accel_ref):
    lines, segments = offset_ref.shape[1:]
    shape = (lines, segments)
    row_index = lax.broadcasted_iota(jnp.int32, shape, 0)
    node_index = lax.broadcasted_iota(jnp.int32, shape, 1)
    heading = headings(me * lines + row_index)
    depth = (segments - node_index).astype(F32)
    points = [-line_spacing * heading[c] * depth + offset_ref[c] for c in range(3)]
    fair = [jnp.zeros(shape, F32)] * 3
    for line in range(lines):
        owner = lax.bitwise_xor(me, line_platform_ref[line])
        fair = [jnp.where(row_index == line, table_ref[owner, c], fair[c]) for c in range(3)]
    last = node_index == segments - 1
    following = [
        jnp.where(last, fair[c], pltpu.roll(points[c], segments - 1, 1)) for c in range(3)
    ]
    pull = pulls([following[c] - points[c] for c in range(3)])
    for c in range(3):
        previous = jnp.where(node_index == 0, 0.0, pltpu.roll(pull[c], 1, 1))
        gravity = -node_weight if c == 2 else 0.0
        acceleration = pull[c] - previous + gravity - line_damping * line_velocity_ref[c]
        line_accel_ref[c] = jnp.where(node_index == 0, 0.0, acceleration)


def platform_pulls(me, table_ref, misc_ref, lines):
    shape = (misc_ref.shape[0], LANES)
    sender = lax.bitwise_xor(lax.broadcasted_iota(jnp.int32, shape, 0), jnp.full(shape, me))
    number = lax.broadcasted_iota(jnp.int32, shape, 1)
    heading = headings(sender * lines + number)
    ends = [
        table_ref[0, c] - (-line_spacing * heading[c] + misc_row(misc_ref, 9 + c)) for c in range(3)
    ]
    ours = jnp.logical_and(number < lines, misc_row(misc_ref, 12) == me.astype(F32))
    taken = [jnp.where(ours, part, 0.0) for part in pulls(ends)]
    return [jnp.sum(jnp.sum(t, axis=0, keepdims=True), axis=1, keepdims=True) for t in taken]


def first_kernel(
    me_ref,
    table_ref,
    thrust_ref,
    restoring_ref,
    line_platform_ref,
    misc_ref,
    pos_ref,
    history_ref,
    memory_ref,
    offset_ref,
    line_velocity_ref,
    base_ref,
    target_pos_ref,
    state_ref,
    line_accel_ref,
    sums_ref,
    *scratch,
):
    me = me_ref[0]
    own_count = pos_ref.shape[1]
    nodes = platform_nodes(me, misc_ref)
    current = jnp.concatenate([nodes[c : c + 1] + table_ref[0, c] for c in range(3)], axis=0)
    target_pos_ref[:, 0:own_count] = pos_ref[...]
    target_pos_ref[:, own_count : own_count + LANES] = current
    target_pos_ref[:, own_count + LANES :] = current
    sums_ref[...] = jnp.zeros_like(sums_ref)
    own_lines(me, table_ref, line_platform_ref, offset_ref, line_velocity_ref, line_accel_ref)
    pull = platform_pulls(me, table_ref, misc_ref, offset_ref.shape[1])
    history = jnp.concatenate([history_ref[j] for j in range(6)], axis=0)
    state_ref[0:8, :] = nodes
    for i in range(6):
        product = jnp.sum(memory_ref[i] * history, axis=0, keepdims=True)
        value = -jnp.sum(product, axis=1, keepdims=True) - restoring_ref[i] * table_ref[0, i]
        if i < 3:
            value = value - pull[i]
        state_ref[8 + i : 9 + i, :] = jnp.broadcast_to(value, (1, LANES))
    scales = strength_scales(me, table_ref, thrust_ref)
    pair_sums([base_ref], scales, target_pos_ref, sums_ref, scratch)


def middle_kernel(count, me_ref, table_ref, thrust_ref, target_pos_ref, before_ref, *rest):
    block_refs, (sums_ref, *scratch) = rest[:count], rest[count:]
    sums_ref[...] = before_ref[...]
    scales = strength_scales(me_ref[0], table_ref, thrust_ref)
    pair_sums(block_refs, scales, target_pos_ref, sums_ref, scratch)


def last_kernel(
    count, me_ref, table_ref, thrust_ref, mass_ref, target_pos_ref, before_ref, state_ref, *rest
):
    block_refs, (induced_ref, accel_ref, sums_ref, *scratch) = rest[:count], rest[count:]
    sums_ref[...] = before_ref[...]
    scales = strength_scales(me_ref[0], table_ref, thrust_ref)
    pair_sums(block_refs, scales, target_pos_ref, sums_ref, scratch)
    tiles = sums_ref.shape[0]

    def velocity(tile):
        sums = sums_ref[tile]
        at = target_pos_ref[:, tile * TILE : (tile + 1) * TILE]
        a = [sums[c : c + 1] + sums[c + 3 : c + 4] for c in range(3)]
        b = [sums[c + 6 : c + 7] + sums[c + 9 : c + 10] + sums[c + 12 : c + 13] for c in range(3)]
        x = [at[c : c + 1] for c in range(3)]
        return [
            (a[1] * x[2] - a[2] * x[1] - b[0]) * inverse_four_pi,
            (a[2] * x[0] - a[0] * x[2] - b[1]) * inverse_four_pi,
            (a[0] * x[1] - a[1] * x[0] - b[2]) * inverse_four_pi,
        ]

    for tile in range(tiles - 1):
        induced_ref[:, tile * TILE : (tile + 1) * TILE] = jnp.concatenate(velocity(tile), axis=0)

    wind = [row[:, 0:LANES] for row in velocity(tiles - 1)]
    arm = [state_ref[3 + c : 4 + c, :] for c in range(3)]
    turn = [table_ref[0, 9 + c] for c in range(3)]
    rigid = [
        table_ref[0, 6] + (turn[1] * arm[2] - turn[2] * arm[1]),
        table_ref[0, 7] + (turn[2] * arm[0] - turn[0] * arm[2]),
        table_ref[0, 8] + (turn[0] * arm[1] - turn[1] * arm[0]),
    ]
    relative = [1.0 + wind[0] - rigid[0], wind[1] - rigid[1], wind[2] - rigid[2]]
    magnitude = jnp.sqrt(
        relative[0] * relative[0] + relative[1] * relative[1] + relative[2] * relative[2]
    )
    force = [state_ref[6:7, :] * magnitude * row for row in relative]
    moment = [
        arm[1] * force[2] - arm[2] * force[1],
        arm[2] * force[0] - arm[0] * force[2],
        arm[0] * force[1] - arm[1] * force[0],
    ]
    total = [
        jnp.sum(row, axis=1, keepdims=True) + state_ref[8 + i : 9 + i, 0:1]
        for i, row in enumerate(force + moment)
    ]
    lane = lax.broadcasted_iota(jnp.int32, (1, LANES), 1)
    result = jnp.zeros((1, LANES), F32)
    for i in range(6):
        value = mass_ref[i, 0] * total[0]
        for j in range(1, 6):
            value = value + mass_ref[i, j] * total[j]
        result = jnp.where(lane == i, value, result)
    accel_ref[...] = result[:, 0:6]


def shards(
    particle_pos,
    vorticity,
    particle_owner,
    thrust_coef,
    node_pos,
    lever_arm,
    chord_coef,
    node_platform,
    platform_pos,
    platform_vel,
    velocity_history,
    memory_kernel,
    restoring,
    inverse_mass,
    line_offset,
    line_velocity,
    line_platform,
):
    devices = lax.axis_size("blk")
    me = lax.axis_index("blk")
    own_count = particle_pos.shape[1]
    tiles = own_count // TILE + 1

    smem = pl.BlockSpec(memory_space=pltpu.SMEM)
    vmem = pl.BlockSpec(memory_space=pltpu.VMEM)
    own = pl.pallas_call(
        pack_kernel,
        in_specs=[smem] + [vmem] * 10,
        out_specs=vmem,
        out_shape=jax.ShapeDtypeStruct((1, 8, own_count), F32),
        name="pack",
    )(
        line_platform,
        particle_pos,
        vorticity,
        particle_owner[None],
        node_pos,
        lever_arm,
        chord_coef[None],
        node_platform[None],
        platform_pos.T,
        platform_vel.T,
        line_offset,
    )

    def swap(values, distance):
        return lax.ppermute(values, "blk", [(i, i ^ distance) for i in range(devices)])

    base = jnp.concatenate([own, swap(own, 1)], axis=0)
    base = jnp.concatenate([base, swap(base, 2)], axis=0)
    misc = base[:, 7, :]
    distance = 4
    while distance < devices:
        misc = jnp.concatenate([misc, swap(misc, distance)], axis=0)
        distance *= 2
    misc, base = lax.optimization_barrier((misc, base))
    far = swap(base, 4)
    table = misc[:, 8 * LANES : 8 * LANES + 16]

    sums_shape = jax.ShapeDtypeStruct((tiles, 16, TILE), F32)

    def call(kernel, scalars, arrays, blocks, out_shape):
        count = sum(block.shape[0] for block in blocks)
        rows = count * own_count // QUARTERS
        reach = next(r for r in (1024, 512) if rows % r == 0)
        work = count * own_count * (tiles * TILE - LANES)
        return pl.pallas_call(
            kernel,
            in_specs=[smem] * len(scalars) + [vmem] * (len(arrays) + len(blocks)),
            out_specs=(vmem,) * len(out_shape),
            out_shape=out_shape,
            scratch_shapes=[
                pltpu.VMEM((rows, LANES), BF16),
                pltpu.VMEM((QUARTERS, 16, rows), BF16),
                pltpu.VMEM((tiles * QUARTERS, LANES, TILE), BF16),
                pltpu.VMEM((QUARTERS * reach, TILE), F32),
                pltpu.VMEM((QUARTERS * reach, TILE), F32),
            ],
            compiler_params=pltpu.CompilerParams(vmem_limit_bytes=48 * 2**20),
            cost_estimate=pl.CostEstimate(
                flops=1200 * work, bytes_accessed=count * own_count * 32, transcendentals=0
            ),
            name="pairs",
        )(*scalars, *arrays, *blocks)

    me = me.astype(jnp.int32)[None]
    target_pos, state, line_accel, sums = call(
        first_kernel,
        [me, table, thrust_coef, restoring, line_platform],
        [misc, particle_pos, jnp.transpose(velocity_history, (1, 0, 2)), memory_kernel]
        + [line_offset, line_velocity],
        [base],
        (
            jax.ShapeDtypeStruct((3, tiles * TILE), F32),
            jax.ShapeDtypeStruct((16, LANES), F32),
            jax.ShapeDtypeStruct(line_offset.shape, F32),
            sums_shape,
        ),
    )
    distance = 8
    while distance < devices:
        sums, base, far = lax.optimization_barrier((sums, base, far))
        base = jnp.concatenate([base, far], axis=0)
        blocks, far = far, swap(base, distance)
        (sums,) = call(
            functools.partial(middle_kernel, 1),
            [me, table, thrust_coef],
            [target_pos, sums],
            [blocks],
            (sums_shape,),
        )
        distance *= 2
    induced, accel, unused = call(
        functools.partial(last_kernel, 1),
        [me, table, thrust_coef, inverse_mass],
        [target_pos, sums, state],
        [far],
        (
            jax.ShapeDtypeStruct(particle_pos.shape, F32),
            jax.ShapeDtypeStruct((1, 6), F32),
            sums_shape,
        ),
    )
    return (induced, accel.reshape(6, 1), line_accel)


def solution(mesh):
    return jax.shard_map(
        shards,
        mesh=mesh,
        in_specs=(
            P(None, ("farm", "blk")),
            P(None, ("farm", "blk")),
            P(("farm", "blk")),
            P("farm"),
            P(None, ("farm", "blk")),
            P(None, ("farm", "blk")),
            P(("farm", "blk")),
            P(("farm", "blk")),
            P(None, ("farm", "blk")),
            P(None, ("farm", "blk")),
            P(("farm", "blk"), None, None),
            P(),
            P(),
            P(),
            P(None, ("farm", "blk"), None),
            P(None, ("farm", "blk"), None),
            P(("farm", "blk")),
        ),
        out_specs=(
            P(None, ("farm", "blk")),
            P(None, ("farm", "blk")),
            P(None, ("farm", "blk"), None),
        ),
        check_vma=False,
    )
```

```python
import functools
import math

import jax
import jax.numpy as jnp
import numpy as np
from jax import lax
from jax.experimental import pallas as pl
from jax.experimental.pallas import tpu as pltpu
from jax.sharding import PartitionSpec as P

core_square = 0.01
inverse_four_pi = 0.25 / math.pi
line_spacing = 1.0
rest_length = 0.95 * math.sqrt(1.36)
line_stiffness = 20.0
node_weight = 0.5
line_damping = 0.5
F32 = jnp.float32
BF16 = jnp.bfloat16
LANES = 128
TILE = 256
QUARTERS = 4
FEATURES = 32
SPAN = 256
third_turn = np.float32(2.0 * math.pi / 3.0)
cosines = [float(np.cos(third_turn * np.float32(k))) for k in range(3)]
sines = [float(np.sin(third_turn * np.float32(k))) for k in range(3)]


def piece(values):
    return values.astype(BF16).astype(F32)


def coordinate_pieces(pos, extra):
    first = jnp.round(pos * 64.0) * (1.0 / 64.0)
    rest = pos - first
    second = jnp.round(rest * 16384.0) * (1.0 / 16384.0)
    third = piece(rest - second)
    square = first * first
    norm = square[0:1] + square[1:2] + square[2:3]
    cross = rest * (pos + first)
    small = cross[0:1] + cross[1:2] + cross[2:3] + extra
    norm_a = piece(norm)
    norm_b = norm - norm_a
    small_a = piece(small)
    small_b = small - small_a
    return first, second, third, norm_a, norm_b, small_a, small_b


def source_rows(pos):
    first, second, third, norm_a, norm_b, small_a, small_b = coordinate_pieces(pos, 0.0)
    one = jnp.ones_like(norm_a)
    return jnp.concatenate(
        [first, norm_a, one, norm_b, one, small_a, one, first, second, small_b, one]
        + [second, first, third, second, third],
        axis=0,
    )


def target_rows(pos):
    first, second, third, norm_a, norm_b, small_a, small_b = coordinate_pieces(pos, core_square)
    one = jnp.ones_like(norm_a)
    first, second, third = -2.0 * first, -2.0 * second, -2.0 * third
    return jnp.concatenate(
        [first, one, norm_a, one, norm_b, one, small_a, second, first, one, small_b]
        + [second, third, first, third, second],
        axis=0,
    )


def strength_rows(block, scale):
    pos, vorticity = block[0:3], block[3:6]
    strength = vorticity * scale
    s_hi = piece(strength)
    s_lo = piece(strength - s_hi)
    held = s_hi + s_lo
    moment = jnp.concatenate(
        [
            held[1:2] * pos[2:3] - held[2:3] * pos[1:2],
            held[2:3] * pos[0:1] - held[0:1] * pos[2:3],
            held[0:1] * pos[1:2] - held[1:2] * pos[0:1],
        ],
        axis=0,
    )
    m_hi = piece(moment)
    m_mid = piece(moment - m_hi)
    m_lo = moment - m_hi - m_mid
    return jnp.concatenate([s_hi, s_lo, m_hi, m_mid, m_lo, jnp.zeros_like(scale)], axis=0)


def strength_scales(me, table_ref, thrust_ref):
    return [
        thrust_ref[index] * (1.0 - table_ref[lax.bitwise_xor(me, index), 6])
        for index in range(thrust_ref.shape[0])
    ]


def pair_sums(block_refs, scales, target_pos_ref, sums_ref, scratch):
    rows_ref, weights_ref, targets_ref, even_ref, odd_ref, scale_ref = scratch
    quarter = block_refs[0].shape[2] // QUARTERS
    tiles = sums_ref.shape[0] - 1
    halves = QUARTERS // 2
    for tile in range(tiles):
        features = target_rows(target_pos_ref[:, tile * TILE : (tile + 1) * TILE]).astype(BF16)
        for part in range(QUARTERS):
            slot = targets_ref.at[tile * QUARTERS + part]
            slot[...] = jnp.zeros((LANES, TILE), BF16)
            slot[part * FEATURES : (part + 1) * FEATURES, :] = features
    features = target_rows(target_pos_ref[:, tiles * TILE : (tiles + 1) * TILE]).astype(BF16)
    left = features[:, 0:LANES]
    for half in range(halves):
        slot = targets_ref.at[tiles * QUARTERS + half]
        slot[...] = jnp.zeros((LANES, TILE), BF16)
        for side in range(2):
            part = 2 * half + side
            slot[part * FEATURES : (part + 1) * FEATURES, side * LANES : (side + 1) * LANES] = left

    first = 0
    for block_ref in block_refs:
        owner = block_ref[:, 6, :]
        scale = jnp.zeros_like(owner)
        for index, value in enumerate(scales):
            scale = jnp.where(owner == float(index), value, scale)
        scale_ref[first : first + block_ref.shape[0], :] = scale

        def prepare(index, carry, block_ref=block_ref, first=first):
            block = block_ref[index]
            features = source_rows(block[0:3]).astype(BF16)
            stacked = jnp.concatenate(
                [features[:, part * quarter : (part + 1) * quarter] for part in range(QUARTERS)],
                axis=0,
            )
            start = pl.multiple_of((first + index) * quarter, quarter)
            rows_ref[pl.ds(start, quarter), :] = stacked.T
            strengths = strength_rows(block, scale_ref[pl.ds(first + index, 1), :]).astype(BF16)
            for part in range(QUARTERS):
                weights_ref[part, :, pl.ds(start, quarter)] = strengths[
                    :, part * quarter : (part + 1) * quarter
                ]
            return carry

        lax.fori_loop(0, block_ref.shape[0], prepare, 0, unroll=4)
        first += block_ref.shape[0]

    rows = rows_ref.shape[0]
    reach = even_ref.shape[0] // QUARTERS
    chunks = rows // reach
    steps = tiles * chunks
    span = SPAN

    def distances_into(buffer, at, start, count, features):
        for k in range(0, count, span):
            buffer[at + k : at + k + span, :] = jnp.dot(
                rows_ref[pl.ds(start + k, span), :], features, preferred_element_type=F32
            )

    def summed(buffer, at, weights):
        root = lax.rsqrt(buffer[at : at + span, :])
        pair = root * root * root
        high = pair.astype(BF16)
        low = (pair - high.astype(F32)).astype(BF16)
        return jnp.dot(weights, high, preferred_element_type=F32) + jnp.dot(
            weights, low, preferred_element_type=F32
        )

    def distances(step, buffer):
        tile = step // chunks
        start = pl.multiple_of(step % chunks * reach, reach)
        for part in range(QUARTERS):
            features = targets_ref[tile * QUARTERS + part]
            distances_into(buffer, part * reach, start, reach, features)

    def add_up(step, buffer):
        tile = step // chunks
        start = pl.multiple_of(step % chunks * reach, reach)
        total = jnp.zeros((16, TILE), F32)
        for part in range(QUARTERS):
            for k in range(0, reach, span):
                weights = weights_ref[part, :, pl.ds(start + k, span)]
                total = total + summed(buffer, part * reach + k, weights)
        sums_ref[tile] += total

    node_reach = min(rows, 2 * reach)

    def node_distances(start, buffer):
        for half in range(halves):
            features = targets_ref[tiles * QUARTERS + half]
            distances_into(buffer, half * node_reach, start, node_reach, features)

    def node_add_up(start, buffer):
        total = jnp.zeros((32, TILE), F32)
        for half in range(halves):
            for k in range(0, node_reach, span):
                weights = weights_ref[2 * half : 2 * half + 2, :, pl.ds(start + k, span)]
                weights = weights.reshape(32, span)
                total = total + summed(buffer, half * node_reach + k, weights)
        sums_ref[tiles, :, 0:LANES] += total[0:16, 0:LANES] + total[16:32, LANES:]

    def two_steps(index, carry):
        step = 2 * index
        distances(step + 1, odd_ref)
        add_up(step, even_ref)
        distances(step + 2, even_ref)
        add_up(step + 1, odd_ref)
        return carry

    distances(0, even_ref)
    doubles = (steps - 1) // 2
    lax.fori_loop(0, doubles, two_steps, 0)
    stages = [(functools.partial(distances, k), functools.partial(add_up, k)) for k in range(2 * doubles, steps)]
    stages += [
        (functools.partial(node_distances, start), functools.partial(node_add_up, start))
        for start in range(0, rows, node_reach)
    ]
    buffers = [even_ref, odd_ref]
    for index, (unused, add) in enumerate(stages):
        if index + 1 < len(stages):
            stages[index + 1][0](buffers[(index + 1) % 2])
        add(buffers[index % 2])


def misc_row(misc_ref, row):
    return misc_ref[:, row * LANES : (row + 1) * LANES]


def pack_kernel(
    line_platform_ref,
    pos_ref,
    vorticity_ref,
    owner_ref,
    node_pos_ref,
    lever_arm_ref,
    chord_ref,
    node_platform_ref,
    platform_pos_ref,
    platform_vel_ref,
    offset_ref,
    own_ref,
):
    own_ref[0, 0:3, :] = pos_ref[...]
    own_ref[0, 3:6, :] = vorticity_ref[...]
    own_ref[0, 6:7, :] = owner_ref[...].astype(F32)
    own_ref[0, 7:8, :] = jnp.zeros(owner_ref.shape, F32)

    def put(row, values):
        own_ref[0, 7:8, row * LANES : row * LANES + values.shape[1]] = values

    lane = lax.broadcasted_iota(jnp.int32, (1, LANES), 1)
    for c in range(3):
        put(c, node_pos_ref[c : c + 1, :])
        put(3 + c, lever_arm_ref[c : c + 1, :])
        row = jnp.zeros((1, LANES), F32)
        for line in range(offset_ref.shape[1]):
            row = jnp.where(lane == line, offset_ref[c, line : line + 1, LANES - 1 :], row)
        put(9 + c, row)
    put(6, chord_ref[...])
    put(7, node_platform_ref[...].astype(F32))
    put(8, jnp.concatenate([platform_pos_ref[...], platform_vel_ref[...]], axis=1))
    row = jnp.zeros((1, LANES), F32)
    for line in range(offset_ref.shape[1]):
        row = jnp.where(lane == line, line_platform_ref[line].astype(F32), row)
    put(12, row)


def platform_nodes(me, misc_ref):
    devices = misc_ref.shape[0]
    on_platform = misc_row(misc_ref, 7) == me.astype(F32)
    mark = on_platform.astype(F32)
    upper = lax.broadcasted_iota(jnp.int32, (LANES, LANES), 0) <= lax.broadcasted_iota(
        jnp.int32, (LANES, LANES), 1
    )
    counted = jnp.dot(mark.astype(BF16), upper.astype(F32).astype(BF16), preferred_element_type=F32)
    below = lax.broadcasted_iota(jnp.int32, (devices, devices), 0) > lax.broadcasted_iota(
        jnp.int32, (devices, devices), 1
    )
    totals = jnp.broadcast_to(counted[:, LANES - 1 :], counted.shape)
    before = jnp.dot(below.astype(F32).astype(BF16), totals.astype(BF16), preferred_element_type=F32)
    rank = jnp.where(on_platform, counted - 1.0 + before, -1.0)
    slots = lax.broadcasted_iota(jnp.int32, (LANES, LANES), 0).astype(F32)
    picked = jnp.zeros((24, LANES), F32)
    for device in range(devices):
        data = jnp.concatenate(
            [misc_ref[device : device + 1, k * LANES : (k + 1) * LANES] for k in range(8)], axis=0
        )
        hi = piece(data)
        mid = piece(data - hi)
        pieces = jnp.concatenate([hi, mid, data - hi - mid], axis=0).astype(BF16)
        pick = (slots == rank[device : device + 1]).astype(F32).astype(BF16)
        picked = picked + lax.dot_general(
            pieces, pick, (((1,), (1,)), ((), ())), preferred_element_type=F32
        )
    return picked[0:8] + picked[8:16] + picked[16:24]


def headings(number):
    which = lax.rem(number, 3)
    pick = lambda values: jnp.where(
        which == 0, values[0], jnp.where(which == 1, values[1], values[2])
    )
    return [pick(cosines), pick(sines), jnp.full(number.shape, 0.6, F32)]


def pulls(segment):
    length = jnp.sqrt(segment[0] * segment[0] + segment[1] * segment[1] + segment[2] * segment[2])
    tension = line_stiffness * (length - rest_length) / rest_length
    return [tension / length * part for part in segment]


def own_lines(me, table_ref, line_platform_ref, offset_ref, line_velocity_ref, line_accel_ref):
    lines, segments = offset_ref.shape[1:]
    shape = (lines, segments)
    row_index = lax.broadcasted_iota(jnp.int32, shape, 0)
    node_index = lax.broadcasted_iota(jnp.int32, shape, 1)
    heading = headings(me * lines + row_index)
    depth = (segments - node_index).astype(F32)
    points = [-line_spacing * heading[c] * depth + offset_ref[c] for c in range(3)]
    fair = [jnp.zeros(shape, F32)] * 3
    for line in range(lines):
        owner = lax.bitwise_xor(me, line_platform_ref[line])
        fair = [jnp.where(row_index == line, table_ref[owner, c], fair[c]) for c in range(3)]
    last = node_index == segments - 1
    following = [
        jnp.where(last, fair[c], pltpu.roll(points[c], segments - 1, 1)) for c in range(3)
    ]
    pull = pulls([following[c] - points[c] for c in range(3)])
    for c in range(3):
        previous = jnp.where(node_index == 0, 0.0, pltpu.roll(pull[c], 1, 1))
        gravity = -node_weight if c == 2 else 0.0
        acceleration = pull[c] - previous + gravity - line_damping * line_velocity_ref[c]
        line_accel_ref[c] = jnp.where(node_index == 0, 0.0, acceleration)


def platform_pulls(me, table_ref, misc_ref, lines):
    shape = (misc_ref.shape[0], LANES)
    sender = lax.bitwise_xor(lax.broadcasted_iota(jnp.int32, shape, 0), jnp.full(shape, me))
    number = lax.broadcasted_iota(jnp.int32, shape, 1)
    heading = headings(sender * lines + number)
    ends = [
        table_ref[0, c] - (-line_spacing * heading[c] + misc_row(misc_ref, 9 + c)) for c in range(3)
    ]
    ours = jnp.logical_and(number < lines, misc_row(misc_ref, 12) == me.astype(F32))
    taken = [jnp.where(ours, part, 0.0) for part in pulls(ends)]
    return [jnp.sum(jnp.sum(t, axis=0, keepdims=True), axis=1, keepdims=True) for t in taken]


def first_kernel(
    me_ref,
    table_ref,
    thrust_ref,
    restoring_ref,
    line_platform_ref,
    misc_ref,
    history_ref,
    memory_ref,
    offset_ref,
    line_velocity_ref,
    base_ref,
    target_pos_ref,
    state_ref,
    line_accel_ref,
    sums_ref,
    *scratch,
):
    me = me_ref[0]
    own_count = base_ref.shape[2]
    nodes = platform_nodes(me, misc_ref)
    current = jnp.concatenate([nodes[c : c + 1] + table_ref[0, c] for c in range(3)], axis=0)
    target_pos_ref[:, 0:own_count] = base_ref[0, 0:3, :]
    target_pos_ref[:, own_count : own_count + LANES] = current
    target_pos_ref[:, own_count + LANES :] = current
    sums_ref[...] = jnp.zeros_like(sums_ref)
    own_lines(me, table_ref, line_platform_ref, offset_ref, line_velocity_ref, line_accel_ref)
    pull = platform_pulls(me, table_ref, misc_ref, offset_ref.shape[1])
    history = jnp.concatenate([history_ref[j] for j in range(6)], axis=0)
    state_ref[0:8, :] = nodes
    for i in range(6):
        product = jnp.sum(memory_ref[i] * history, axis=0, keepdims=True)
        value = -jnp.sum(product, axis=1, keepdims=True) - restoring_ref[i] * table_ref[0, i]
        if i < 3:
            value = value - pull[i]
        state_ref[8 + i : 9 + i, :] = jnp.broadcast_to(value, (1, LANES))
    scales = strength_scales(me, table_ref, thrust_ref)
    pair_sums([base_ref], scales, target_pos_ref, sums_ref, scratch)


def middle_kernel(count, me_ref, table_ref, thrust_ref, target_pos_ref, before_ref, *rest):
    block_refs, (sums_ref, *scratch) = rest[:count], rest[count:]
    sums_ref[...] = before_ref[...]
    scales = strength_scales(me_ref[0], table_ref, thrust_ref)
    pair_sums(block_refs, scales, target_pos_ref, sums_ref, scratch)


def last_kernel(
    count, me_ref, table_ref, thrust_ref, mass_ref, target_pos_ref, before_ref, state_ref, *rest
):
    block_refs, (induced_ref, accel_ref, sums_ref, *scratch) = rest[:count], rest[count:]
    sums_ref[...] = before_ref[...]
    scales = strength_scales(me_ref[0], table_ref, thrust_ref)
    pair_sums(block_refs, scales, target_pos_ref, sums_ref, scratch)
    tiles = sums_ref.shape[0]

    def velocity(tile):
        sums = sums_ref[tile]
        at = target_pos_ref[:, tile * TILE : (tile + 1) * TILE]
        a = [sums[c : c + 1] + sums[c + 3 : c + 4] for c in range(3)]
        b = [sums[c + 6 : c + 7] + sums[c + 9 : c + 10] + sums[c + 12 : c + 13] for c in range(3)]
        x = [at[c : c + 1] for c in range(3)]
        return [
            (a[1] * x[2] - a[2] * x[1] - b[0]) * inverse_four_pi,
            (a[2] * x[0] - a[0] * x[2] - b[1]) * inverse_four_pi,
            (a[0] * x[1] - a[1] * x[0] - b[2]) * inverse_four_pi,
        ]

    for tile in range(tiles - 1):
        induced_ref[:, tile * TILE : (tile + 1) * TILE] = jnp.concatenate(velocity(tile), axis=0)

    wind = [row[:, 0:LANES] for row in velocity(tiles - 1)]
    arm = [state_ref[3 + c : 4 + c, :] for c in range(3)]
    turn = [table_ref[0, 9 + c] for c in range(3)]
    rigid = [
        table_ref[0, 6] + (turn[1] * arm[2] - turn[2] * arm[1]),
        table_ref[0, 7] + (turn[2] * arm[0] - turn[0] * arm[2]),
        table_ref[0, 8] + (turn[0] * arm[1] - turn[1] * arm[0]),
    ]
    relative = [1.0 + wind[0] - rigid[0], wind[1] - rigid[1], wind[2] - rigid[2]]
    magnitude = jnp.sqrt(
        relative[0] * relative[0] + relative[1] * relative[1] + relative[2] * relative[2]
    )
    force = [state_ref[6:7, :] * magnitude * row for row in relative]
    moment = [
        arm[1] * force[2] - arm[2] * force[1],
        arm[2] * force[0] - arm[0] * force[2],
        arm[0] * force[1] - arm[1] * force[0],
    ]
    total = [
        jnp.sum(row, axis=1, keepdims=True) + state_ref[8 + i : 9 + i, 0:1]
        for i, row in enumerate(force + moment)
    ]
    lane = lax.broadcasted_iota(jnp.int32, (1, LANES), 1)
    result = jnp.zeros((1, LANES), F32)
    for i in range(6):
        value = mass_ref[i, 0] * total[0]
        for j in range(1, 6):
            value = value + mass_ref[i, j] * total[j]
        result = jnp.where(lane == i, value, result)
    accel_ref[...] = result[:, 0:6]


def shards(
    particle_pos,
    vorticity,
    particle_owner,
    thrust_coef,
    node_pos,
    lever_arm,
    chord_coef,
    node_platform,
    platform_pos,
    platform_vel,
    velocity_history,
    memory_kernel,
    restoring,
    inverse_mass,
    line_offset,
    line_velocity,
    line_platform,
):
    devices = lax.axis_size("blk")
    me = lax.axis_index("blk")
    own_count = particle_pos.shape[1]
    tiles = own_count // TILE + 1

    smem = pl.BlockSpec(memory_space=pltpu.SMEM)
    vmem = pl.BlockSpec(memory_space=pltpu.VMEM)
    own = pl.pallas_call(
        pack_kernel,
        in_specs=[smem] + [vmem] * 10,
        out_specs=vmem,
        out_shape=jax.ShapeDtypeStruct((1, 8, own_count), F32),
        name="pack",
    )(
        line_platform,
        particle_pos,
        vorticity,
        particle_owner[None],
        node_pos,
        lever_arm,
        chord_coef[None],
        node_platform[None],
        platform_pos.T,
        platform_vel.T,
        line_offset,
    )

    def swap(values, distance):
        return lax.ppermute(values, "blk", [(i, i ^ distance) for i in range(devices)])

    base = jnp.concatenate([own, swap(own, 1)], axis=0)
    base = jnp.concatenate([base, swap(base, 2)], axis=0)
    misc = base[:, 7, :]
    distance = 4
    while distance < devices:
        misc = jnp.concatenate([misc, swap(misc, distance)], axis=0)
        distance *= 2
    misc, base = lax.optimization_barrier((misc, base))
    far = swap(base, 4)
    table = misc[:, 8 * LANES : 8 * LANES + 16]

    sums_shape = jax.ShapeDtypeStruct((tiles, 16, TILE), F32)

    def call(kernel, scalars, arrays, blocks, out_shape):
        count = sum(block.shape[0] for block in blocks)
        rows = count * own_count // QUARTERS
        reach = next(r for r in (2048, 1024, 512) if rows % r == 0)
        work = count * own_count * (tiles * TILE - LANES)
        return pl.pallas_call(
            kernel,
            in_specs=[smem] * len(scalars) + [vmem] * (len(arrays) + len(blocks)),
            out_specs=(vmem,) * len(out_shape),
            out_shape=out_shape,
            scratch_shapes=[
                pltpu.VMEM((rows, LANES), BF16),
                pltpu.VMEM((QUARTERS, 16, rows), BF16),
                pltpu.VMEM((tiles * QUARTERS, LANES, TILE), BF16),
                pltpu.VMEM((QUARTERS * reach, TILE), F32),
                pltpu.VMEM((QUARTERS * reach, TILE), F32),
                pltpu.VMEM((count, own_count), F32),
            ],
            compiler_params=pltpu.CompilerParams(vmem_limit_bytes=48 * 2**20),
            cost_estimate=pl.CostEstimate(
                flops=1200 * work, bytes_accessed=count * own_count * 32, transcendentals=0
            ),
            name="pairs",
        )(*scalars, *arrays, *blocks)

    me = me.astype(jnp.int32)[None]
    target_pos, state, line_accel, sums = call(
        first_kernel,
        [me, table, thrust_coef, restoring, line_platform],
        [misc, jnp.transpose(velocity_history, (1, 0, 2)), memory_kernel]
        + [line_offset, line_velocity],
        [base],
        (
            jax.ShapeDtypeStruct((3, tiles * TILE), F32),
            jax.ShapeDtypeStruct((16, LANES), F32),
            jax.ShapeDtypeStruct(line_offset.shape, F32),
            sums_shape,
        ),
    )
    distance = 8
    while distance < devices:
        sums, base, far = lax.optimization_barrier((sums, base, far))
        base = jnp.concatenate([base, far], axis=0)
        blocks, far = far, swap(base, distance)
        (sums,) = call(
            functools.partial(middle_kernel, 1),
            [me, table, thrust_coef],
            [target_pos, sums],
            [blocks],
            (sums_shape,),
        )
        distance *= 2
    induced, accel, unused = call(
        functools.partial(last_kernel, 1),
        [me, table, thrust_coef, inverse_mass],
        [target_pos, sums, state],
        [far],
        (
            jax.ShapeDtypeStruct(particle_pos.shape, F32),
            jax.ShapeDtypeStruct((1, 6), F32),
            sums_shape,
        ),
    )
    return (induced, accel.reshape(6, 1), line_accel)


def solution(mesh):
    return jax.shard_map(
        shards,
        mesh=mesh,
        in_specs=(
            P(None, ("farm", "blk")),
            P(None, ("farm", "blk")),
            P(("farm", "blk")),
            P("farm"),
            P(None, ("farm", "blk")),
            P(None, ("farm", "blk")),
            P(("farm", "blk")),
            P(("farm", "blk")),
            P(None, ("farm", "blk")),
            P(None, ("farm", "blk")),
            P(("farm", "blk"), None, None),
            P(),
            P(),
            P(),
            P(None, ("farm", "blk"), None),
            P(None, ("farm", "blk"), None),
            P(("farm", "blk")),
        ),
        out_specs=(
            P(None, ("farm", "blk")),
            P(None, ("farm", "blk")),
            P(None, ("farm", "blk"), None),
        ),
        check_vma=False,
    )
```
